256 devices in a mesh: range: 64 (over y, z, core), chan: 4 (over x).
Axes of the slice: x: 4, y: 4, z: 8, core: 2. Of those that a mesh axis runs over, the one named last changes fastest.
Arguments:
- features: bfloat16 [256, 65536], P('chan', 'range'), may hold values from -6 to 6
- hilbert_rank: int32 [65536], P('range'), may hold values from 0 to 65535, as said below
- neighbours: int32 [27, 65536], P(None, 'range'), may hold values from -1 to 512, as said below
- qkv_weight: bfloat16 [3, 256, 256], P(None, None, 'chan')
- out_weight: bfloat16 [256, 256], P(None, 'chan'), may hold values from -0.375 to 0.375
- conv_weight: bfloat16 [27, 256, 256], P(None, 'chan'), may hold values from -0.109375 to 0.109375
- up_weight: bfloat16 [256, 1024], P(None, 'chan'), may hold values from -0.375 to 0.375
- down_weight: bfloat16 [1024, 256], P('chan'), may hold values from -0.1875 to 0.1875
Outputs:
- restored: bfloat16 [256, 65536], P('chan', 'range')
The draws below stay inside these ranges and needn't reach their ends.
Inputs may be any that keep to these rules, and one draw needn't show every extreme that they name: `hilbert_rank`: A permutation of the voxels. The owner of rank r is range r // 1024; the rows of one range device send at most 32 voxels to one owner, and exactly 32 in some pairs of every draw. `neighbours`: row 13 is 256 (the voxel itself); every entry that is not -1 names a rank of the grid, and both 0 and 512 occur.
All inputs are finite; a program needn't handle non-finite values.
Results may differ from the reference program's by a relative error of at most 0.012.
The reference program's roundings to bfloat16 on the way count: a program that leaves them out, or rounds other values in their place, can miss the bound.
Values may be sent and summed in bfloat16 or wider, within the bound.
No kernel may reach another device: no remote copies, remote signals or barrier semaphores. Data moves between devices by JAX's collectives and lax.ppermute only.
A program may use at most 64 MiB of HBM per device.

```python
import jax
import jax.numpy as jnp
from jax import lax

C = 256
H = 16
PATCH = 1024
HD = 16
HID = 1024
KER = 27
HW = 256
PTS_DEV = 1024
TOTAL = 65536
N_RANGE = 64


def draw_hilbert_rank(key, part):
    key = jax.random.fold_in(key, 11)
    key_u, key_v, key_share, key_dest, key_rows = jax.random.split(key, 5)
    groups = N_RANGE
    base = PTS_DEV // N_RANGE
    lane = jnp.arange(groups, dtype=jnp.int32) % 4
    first_pattern = jnp.array([1, -1, 0, 0], jnp.int32)[lane]
    second_pattern = jnp.array([1, 0, -1, 0], jnp.int32)[lane]
    sender = first_pattern[jax.random.permutation(key_u, groups)]
    order_d = jax.random.permutation(key_v, groups)
    recv_one = first_pattern[order_d]
    recv_two = second_pattern[order_d]
    share = jax.random.randint(key_share, (), 1, base, dtype=jnp.int32)
    counts = base + share * sender[:, None] * recv_one[None, :] + (base - share) * sender[:, None] * recv_two[None, :]
    row_end = jnp.cumsum(counts, axis=1)
    row_start = row_end - counts
    col_start = jnp.cumsum(counts, axis=0) - counts
    positions = jnp.arange(PTS_DEV, dtype=jnp.int32)

    def one_source(source):
        dests = jnp.sum((positions[:, None] >= row_end[source][None, :]).astype(jnp.int32), axis=1)
        slot = positions - row_start[source][dests]
        return (dests, col_start[source][dests] + slot)
    dests, offsets = jax.vmap(one_source)(jnp.arange(groups, dtype=jnp.int32))
    dest_keys = jax.random.split(key_dest, groups)
    dest_order = jax.vmap(lambda kk: jax.random.permutation(kk, PTS_DEV))(dest_keys).astype(jnp.int32)
    local = dest_order[dests, offsets]
    ranks = dests * PTS_DEV + local
    row_keys = jax.random.split(key_rows, groups)
    shuffle = jax.vmap(lambda kk: jax.random.permutation(kk, PTS_DEV))(row_keys).astype(jnp.int32)
    ranks = jnp.take_along_axis(ranks, shuffle, axis=1)
    return ranks.reshape(-1).astype(jnp.int32)


def draw_neighbours(key, part):
    key = jax.random.fold_in(key, 23)
    key_delta, key_keep = jax.random.split(key)
    own = jnp.arange(TOTAL, dtype=jnp.int32)[None, :]
    offset = jnp.arange(KER, dtype=jnp.int32)[:, None]
    delta = jax.random.randint(key_delta, (KER, TOTAL), -HW, HW + 1, dtype=jnp.int32)
    keep = jax.random.randint(key_keep, (KER, TOTAL), 0, 2, dtype=jnp.int32) == 1
    marked = own % PTS_DEV == PTS_DEV // 2
    delta = jnp.where(marked & (offset == 0), -HW, delta)
    delta = jnp.where(marked & (offset == KER - 1), HW, delta)
    keep = keep | marked & ((offset == 0) | (offset == KER - 1))
    target = own + delta
    valid = keep & (target >= 0) & (target < TOTAL)
    coded = jnp.where(valid, delta + HW, -1)
    coded = jnp.where(offset == KER // 2, HW + 0 * delta, coded)
    return coded.astype(jnp.int32)


def draw_qkv_weight(key, part):
    key = jax.random.fold_in(key, 37)
    scales = jnp.array([2.5, 2.5, 1.0], jnp.float32)
    values = jax.random.normal(key, (3, C, C), jnp.float32)
    values = jnp.clip(values, -6.0, 6.0)
    return (values * scales[:, None, None] / jnp.sqrt(jnp.float32(C))).astype(jnp.bfloat16)


def block_levels(key, dims, cuts, least, top_value):
    def one(position, parts):
        steps = jax.random.uniform(jax.random.fold_in(jax.random.fold_in(key, 6), position), (parts,), jnp.float32, least / len(cuts), top_value / len(cuts))
        return jnp.repeat(jnp.exp(steps), dims[position] // parts).reshape((-1,) + (1,) * (len(dims) - position - 1))

    loudness = one(*cuts[0])
    for cut in cuts[1:]:
        loudness = loudness * one(*cut)
    return loudness


def scatter_about(key, dims, spread, bound, cuts=(), kind=jnp.bfloat16):
    values = spread * jax.random.normal(key, dims, jnp.float32)
    if cuts:
        values = values * block_levels(key, dims, cuts, -0.22, 0.18)
    return jnp.clip(values, -bound, bound).astype(kind)


def setup_inputs(seed: int = 0) -> dict:
    seeds = jax.random.split(jax.random.key(seed), 9)
    features = scatter_about(seeds[0], (C, TOTAL), 1.0, 6.0, ((0, 4), (1, 64)))
    hilbert_rank = draw_hilbert_rank(jax.random.fold_in(seeds[8], 71), 0)
    neighbours = draw_neighbours(jax.random.fold_in(seeds[8], 71), 0)
    qkv_weight = draw_qkv_weight(jax.random.fold_in(seeds[8], 71), 0)
    out_weight = scatter_about(seeds[4], (C, C), C ** -0.5, 0.375, ((1, 4),))
    conv_weight = scatter_about(seeds[5], (KER, C, C), (KER * C // 2) ** -0.5, 0.109375, ((1, 4),))
    up_weight = scatter_about(seeds[6], (C, HID), C ** -0.5, 0.375, ((1, 4),))
    down_weight = scatter_about(seeds[7], (HID, C), HID ** -0.5, 0.1875, ((0, 4),))
    return {"features": features, "hilbert_rank": hilbert_rank, "neighbours": neighbours, "qkv_weight": qkv_weight, "out_weight": out_weight, "conv_weight": conv_weight, "up_weight": up_weight, "down_weight": down_weight}


def layer_norm(values):
    values = values.astype(jnp.float32)
    mean = lax.optimization_barrier(jnp.mean(values, axis=-1, keepdims=True))
    centred = values - mean
    var = lax.optimization_barrier(jnp.mean(centred * centred, axis=-1, keepdims=True))
    return centred * lax.rsqrt(var + 1e-05)

def patch_heads(q, k, v):
    patches = q.shape[0] // PATCH

    def split(t):
        t = t.reshape(patches, PATCH, H, HD)
        return jnp.transpose(t, (0, 2, 1, 3)).reshape(patches * H, PATCH, HD)

    def one_head(items):
        qh, kh, vh = items
        scores = jnp.einsum('qd,kd->qk', qh.astype(jnp.float32), kh.astype(jnp.float32)) / jnp.sqrt(jnp.float32(HD))
        top = lax.optimization_barrier(jnp.max(scores, axis=-1, keepdims=True))
        expo = jnp.exp(scores - top)
        probs = (expo / lax.optimization_barrier(jnp.sum(expo, axis=-1, keepdims=True))).astype(jnp.bfloat16)
        return jnp.dot(probs.astype(jnp.float32), vh.astype(jnp.float32)).astype(jnp.bfloat16)
    outs = lax.map(one_head, (split(q), split(k), split(v)))
    outs = outs.reshape(patches, H, PATCH, HD)
    return jnp.transpose(outs, (0, 2, 1, 3)).reshape(patches * PATCH, H * HD)

def reference(features, hilbert_rank, neighbours, qkv_weight, out_weight, conv_weight, up_weight, down_weight):
    voxels = features.T
    total = voxels.shape[0]
    norm1 = layer_norm(voxels).astype(jnp.bfloat16)
    q = jnp.dot(norm1, qkv_weight[0], preferred_element_type=jnp.float32).astype(jnp.bfloat16)
    k = jnp.dot(norm1, qkv_weight[1], preferred_element_type=jnp.float32).astype(jnp.bfloat16)
    v = jnp.dot(norm1, qkv_weight[2], preferred_element_type=jnp.float32).astype(jnp.bfloat16)
    heads_out = patch_heads(q, k, v)
    first = (voxels.astype(jnp.float32) + jnp.dot(heads_out, out_weight, preferred_element_type=jnp.float32)).astype(jnp.bfloat16)
    grouped = jnp.zeros_like(first).at[hilbert_rank].set(first)
    own = jnp.arange(total, dtype=jnp.int32)[None, :]
    safe = jnp.where(neighbours < 0, total, own + neighbours - HW).astype(jnp.int32)

    def conv_step(acc, items):
        index, kernel = items
        picked = jnp.take(grouped, index, axis=0, mode='fill', fill_value=0)
        return (acc + jnp.dot(picked, kernel.T, preferred_element_type=jnp.float32), None)
    conv, _ = lax.scan(conv_step, jnp.zeros((total, grouped.shape[1]), jnp.float32), (safe, conv_weight))
    second = (grouped.astype(jnp.float32) + conv).astype(jnp.bfloat16)
    norm2 = layer_norm(second).astype(jnp.bfloat16)
    hidden = jax.nn.gelu(jnp.dot(norm2, up_weight, preferred_element_type=jnp.float32), approximate=False).astype(jnp.bfloat16)
    third = (second.astype(jnp.float32) + jnp.dot(hidden, down_weight, preferred_element_type=jnp.float32)).astype(jnp.bfloat16)
    return jnp.take(third, hilbert_rank, axis=0).T
```

```python
import jax
import jax.numpy as jnp
from jax import lax
from jax.experimental import pallas as pl
from jax.experimental.pallas import tpu as pltpu
from jax.sharding import PartitionSpec as P

HD = 16
KER = 27
HW = 256
CHAN = 4
SLOTS = 32
HALF = SLOTS // 2
F32 = jnp.float32
BF16 = jnp.bfloat16

NN = (((1,), (0,)), ((), ()))
NT = (((1,), (1,)), ((), ()))
TN = (((0,), (0,)), ((), ()))


def dot(a, b, dims=NN):
    return lax.dot_general(a, b, dims, preferred_element_type=F32)


def kernel_call(body, outs, cost, operands, scratch=(), vmem=48):
    specs = [pl.BlockSpec(memory_space=pltpu.SMEM if x.shape == (1,) else pltpu.VMEM) for x in operands]
    call = pl.pallas_call(
        body,
        out_shape=outs,
        in_specs=specs,
        scratch_shapes=list(scratch),
        compiler_params=pltpu.CompilerParams(vmem_limit_bytes=vmem * 1024 * 1024),
        cost_estimate=pl.CostEstimate(flops=cost, bytes_accessed=1 << 20, transcendentals=0),
    )
    return call(*operands)


def column_norm(x):
    mean = jnp.mean(x, axis=0, keepdims=True)
    centred = x - mean
    var = jnp.mean(centred * centred, axis=0, keepdims=True)
    return (centred * lax.rsqrt(var + 1e-05)).astype(BF16)


def place_blocks(dst, blocks, me):
    for k, block in enumerate(blocks):
        owner = lax.rem(me + CHAN - k, CHAN)
        size = block.shape[0]
        dst[pl.ds(pl.multiple_of(owner * size, size), size), :] = block[...]


def attention_body(me_ref, x0, x1, x2, x3, w_ref, out_ref, xs, qkv):
    place_blocks(xs, (x0, x1, x2, x3), me_ref[0])
    rows = xs.shape[1]
    norm = column_norm(xs[...].astype(F32))
    proj = dot(w_ref[...], norm)
    width = out_ref.shape[0]
    qkv[0:width, :] = (proj[0:width].astype(BF16) * BF16(0.25)).astype(BF16)
    qkv[width:, :] = proj[width:].astype(BF16)
    ones = (lax.broadcasted_iota(jnp.int32, (HD, rows), 0) == 0).astype(F32).astype(BF16)
    block = 256
    for head in range(width // HD):
        lo = head * HD
        keys = qkv[width + lo : width + lo + HD, :]
        vals = jnp.concatenate([qkv[2 * width + lo : 2 * width + lo + HD, :], ones], axis=0)
        for part in range(rows // block):
            cols = slice(part * block, (part + 1) * block)
            scores = dot(keys, qkv[lo : lo + HD, cols], TN)
            top = jnp.max(scores, axis=0, keepdims=True)
            expo = jnp.exp(scores - top).astype(BF16)
            res = dot(vals, expo)
            out_ref[lo : lo + HD, cols] = (res[0:HD] / res[HD : HD + 1]).astype(BF16)


def slot_match(code, half, start, size, cols):
    rows = lax.broadcasted_iota(jnp.int32, (size, cols), 0) + (start + half * 1024)
    return (rows == code).astype(F32).astype(BF16)


def send_body(me_ref, h0, h1, h2, h3, x_ref, w_ref, code_ref, out_ref, hs):
    place_blocks(hs, (h0, h1, h2, h3), me_ref[0])
    first = (x_ref[...].astype(F32) + dot(w_ref[...], hs[...])).astype(BF16)
    zero = jnp.zeros_like(first)
    low = jnp.concatenate([first, zero], axis=0)
    high = jnp.concatenate([zero, first], axis=0)
    code = code_ref[...]
    block = 256
    for start in range(0, out_ref.shape[0], block):
        res = dot(slot_match(code, 0, start, block, code.shape[1]), low, NT)
        res += dot(slot_match(code, 1, start, block, code.shape[1]), high, NT)
        out_ref[start : start + block, :] = res.astype(BF16)


def group_body(me_ref, got_ref, place_ref, own_ref, m1_ref, m2_ref, m3_ref, first_ref, last_ref, tmp):
    me = me_ref[0]
    width = own_ref.shape[1]
    got = got_ref[...].astype(F32).T.astype(BF16)
    for q in range(CHAN):
        rows = lax.broadcasted_iota(jnp.int32, (256, got.shape[1]), 0) + q * 256
        res = 0.0
        for half in range(2):
            match = (rows == place_ref[half : half + 1, :]).astype(F32).astype(BF16)
            res += dot(got[half * width : (half + 1) * width], match, NT)
        tmp[q] = res.astype(BF16)
    for k, ref in enumerate((own_ref, m1_ref, m2_ref, m3_ref)):
        target = lax.rem(me + k, CHAN)
        for b in range(3):
            ref[b] = tmp[jnp.clip(target - 1 + b, 0, CHAN - 1)]
    first_ref[...] = tmp[0]
    last_ref[...] = tmp[CHAN - 1]


def conv_body(me_ref, *refs):
    msgs = refs[0:4]
    halos = refs[4:8]
    near_ref, conv_ref, up_ref, down_ref = refs[8:12]
    outs = refs[12:16]
    win, acc, third_ref = refs[16:19]
    me = me_ref[0]
    quarter = 64
    for k in range(CHAN):
        owner = lax.rem(me + CHAN - k, CHAN)
        at = pl.ds(pl.multiple_of(owner * quarter, quarter), quarter)
        for b in range(3):
            win[at, b * 256 : (b + 1) * 256] = msgs[k][b]

    @pl.when(me == 0)
    def _():
        for k in range(CHAN):
            win[k * quarter : (k + 1) * quarter, 0:256] = halos[k][...]

    @pl.when(me == CHAN - 1)
    def _():
        for k in range(CHAN):
            src = (k + 1) % CHAN
            win[src * quarter : (src + 1) * quarter, 512:768] = halos[k][...]

    rows = lax.broadcasted_iota(jnp.int32, (768, 256), 0)
    lane = lax.broadcasted_iota(jnp.int32, (1, 256), 1)
    acc[...] = jnp.zeros_like(acc)

    def step(j, carry):
        near = near_ref[pl.ds(j, 1), :]
        target = jnp.where(near < 0, -1, near + lane)
        match = (rows == target).astype(F32).astype(BF16)
        picked = dot(win[...], match).astype(BF16)
        weight = jnp.concatenate([conv_ref[i, j] for i in range(CHAN)], axis=0)
        acc[...] += dot(weight, picked)
        return carry

    lax.fori_loop(0, KER, step, 0)
    second = (win[:, 256:512].astype(F32) + acc[...]).astype(BF16)
    norm = column_norm(second.astype(F32))
    total = second.astype(F32)
    for i in range(CHAN):
        hidden = dot(up_ref[i], norm)
        hidden = (0.5 * hidden * (1.0 + lax.erf(hidden * (2.0 ** -0.5)))).astype(BF16)
        total += dot(down_ref[i], hidden)
    third_ref[...] = total.astype(BF16)
    for k in range(CHAN):
        to = lax.rem(me + k, CHAN)
        outs[k][...] = third_ref[pl.ds(pl.multiple_of(to * quarter, quarter), quarter), :]


def back_body(me_ref, t0, t1, t2, t3, place_ref, out_ref, tmp):
    me = me_ref[0]
    for k, ref in enumerate((t0, t1, t2, t3)):
        tmp[lax.rem(me + CHAN - k, CHAN)] = ref[...]
    third = jnp.concatenate([tmp[q] for q in range(CHAN)], axis=1)
    zero = jnp.zeros_like(third)
    low = jnp.concatenate([third, zero], axis=0)
    high = jnp.concatenate([zero, third], axis=0)
    column = place_ref[...].astype(F32).T
    block = 256
    rank = lax.broadcasted_iota(jnp.int32, (block, third.shape[1]), 1).astype(F32)
    for start in range(0, out_ref.shape[0], block):
        res = 0.0
        for half, rhs in enumerate((low, high)):
            match = (rank == column[start : start + block, half : half + 1]).astype(F32).astype(BF16)
            res += dot(match, rhs, NT)
        out_ref[start : start + block, :] = res.astype(BF16)


def restore_body(got_ref, code_ref, out_ref):
    width = out_ref.shape[0]
    got = got_ref[...].astype(F32).T.astype(BF16)
    code = code_ref[...]
    res = 0.0
    for half in range(2):
        for start in range(0, got.shape[1], 256):
            match = slot_match(code, half, start, 256, code.shape[1])
            res += dot(got[half * width : (half + 1) * width, start : start + 256], match)
    out_ref[...] = res.astype(BF16)


def turn(k):
    return [(i, (i + k) % CHAN) for i in range(CHAN)]


def gather_chan(x):
    return [x] + [lax.ppermute(x, "chan", turn(k)) for k in range(1, CHAN)]


def slot_codes(rank, rows, owners):
    owner = rank // rows
    onehot = (owner[:, None] == jnp.arange(owners, dtype=jnp.int32)[None, :]).astype(F32)
    blocks = onehot.reshape(rows // 128, 128, owners)
    ids = jnp.arange(128, dtype=jnp.int32)
    lower = (ids[:, None] >= ids[None, :]).astype(F32)
    inner = jnp.einsum("ij,bjo->bio", lower, blocks)
    totals = inner[:, -1, :]
    prior = jnp.cumsum(totals, axis=0) - totals
    before = (inner + prior[:, None, :] - 1.0).reshape(rows, owners)
    slot = jnp.sum(onehot * before, axis=1).astype(jnp.int32)
    return (slot // HALF) * 1024 + owner * HALF + slot % HALF


def shards(
    features, hilbert_rank, neighbours, qkv_weight, out_weight, conv_weight, up_weight, down_weight
):
    quarter, rows = features.shape
    owners = lax.axis_size("range")
    me = lax.axis_index("chan").astype(jnp.int32)
    me_ref = me[None]
    sds = jax.ShapeDtypeStruct

    with jax.named_scope("gather_features"):
        blocks = gather_chan(features)
    with jax.named_scope("gather_weights"):
        conv_all = lax.all_gather(conv_weight, "chan", axis=0)
        up_all = lax.all_gather(up_weight.T, "chan", axis=0)
        down_all = lax.all_gather(down_weight.T, "chan", axis=0)

    with jax.named_scope("codes"):
        code = slot_codes(hilbert_rank, rows, owners)
        ids = jnp.arange(2 * rows, dtype=jnp.int32)
        table = jnp.max(
            jnp.where(code[None, :] == ids[:, None], (hilbert_rank % rows)[None, :], -1), axis=1
        )
        tables = lax.all_gather(table, "range", axis=0)
        mine = lax.dynamic_index_in_dim(
            tables.reshape(owners, 2, owners, HALF), lax.axis_index("range"), 2, keepdims=False
        )
        place = jnp.transpose(mine, (1, 0, 2)).reshape(2, rows)
        place = jnp.concatenate([place, jnp.full((6, rows), -1, jnp.int32)], axis=0)
        code = code[None, :]

    qkv = jnp.transpose(qkv_weight, (0, 2, 1)).reshape(3 * quarter, -1)
    with jax.named_scope("attention"):
        heads = kernel_call(
            attention_body,
            sds((quarter, rows), BF16),
            1 << 32,
            [me_ref] + blocks + [qkv],
            [pltpu.VMEM((CHAN * quarter, rows), BF16), pltpu.VMEM((3 * quarter, rows), BF16)],
        )
    with jax.named_scope("gather_heads"):
        blocks = gather_chan(heads)
    with jax.named_scope("send"):
        send = kernel_call(
            send_body,
            sds((owners * HALF, 2 * quarter), BF16),
            1 << 30,
            [me_ref] + blocks + [features, out_weight.T, code],
            [pltpu.VMEM((CHAN * quarter, rows), BF16)],
        )
        got = exchange(send, owners)
    with jax.named_scope("group"):
        part = sds((3, quarter, 256), BF16)
        edge = sds((quarter, 256), BF16)
        own, m1, m2, m3, first_edge, last_edge = kernel_call(
            group_body,
            (part, part, part, part, edge, edge),
            1 << 30,
            [me_ref, got, place],
            [pltpu.VMEM((CHAN, quarter, 256), BF16)],
        )
    with jax.named_scope("gather_window"):
        msgs = [own] + [lax.ppermute(m, "chan", turn(k)) for k, m in ((1, m1), (2, m2), (3, m3))]
        halos = []
        for k in range(CHAN):
            other = (k + 1) % CHAN
            up = [(r * CHAN + k, (r + 1) * CHAN) for r in range(owners - 1)]
            down = [((r + 1) * CHAN + other, r * CHAN + CHAN - 1) for r in range(owners - 1)]
            halos.append(
                lax.ppermute(jnp.where(me == k, last_edge, first_edge), ("range", "chan"), up + down)
            )
    with jax.named_scope("conv_mlp"):
        near = lax.dynamic_slice_in_dim(neighbours, me * 256, 256, 1)
        thirds = kernel_call(
            conv_body,
            (edge, edge, edge, edge),
            1 << 32,
            [me_ref] + msgs + halos + [near, conv_all, up_all, down_all],
            [
                pltpu.VMEM((CHAN * quarter, 768), BF16),
                pltpu.VMEM((CHAN * quarter, 256), F32),
                pltpu.VMEM((CHAN * quarter, 256), BF16),
            ],
        )
    with jax.named_scope("turn_back"):
        thirds = [thirds[0]] + [lax.ppermute(thirds[k], "chan", turn(k)) for k in range(1, CHAN)]
    with jax.named_scope("back"):
        back = kernel_call(
            back_body,
            sds((owners * HALF, 2 * quarter), BF16),
            1 << 30,
            [me_ref] + thirds + [place],
            [pltpu.VMEM((CHAN, quarter, 256), BF16)],
        )
        returned = exchange(back, owners)
    with jax.named_scope("restore"):
        return kernel_call(restore_body, sds((quarter, rows), BF16), 1 << 30, [returned, code])


def exchange(rows, owners):
    parts = rows.reshape(owners, HALF, rows.shape[1])
    parts = lax.all_to_all(parts, "range", split_axis=0, concat_axis=0, tiled=True)
    return parts.reshape(rows.shape)


def solution(mesh):
    in_specs = (
        P("chan", "range"),
        P("range"),
        P(None, "range"),
        P(None, None, "chan"),
        P(None, "chan"),
        P(None, "chan", None),
        P(None, "chan"),
        P("chan", None),
    )
    out_specs = P("chan", "range")
    return jax.shard_map(shards, mesh=mesh, in_specs=in_specs, out_specs=out_specs, check_vma=False)
```

```python
import jax
import jax.numpy as jnp
from jax import lax
from jax.experimental import pallas as pl
from jax.experimental.pallas import tpu as pltpu
from jax.sharding import PartitionSpec as P

HD = 16
KER = 27
HW = 256
CHAN = 4
SLOTS = 32
HALF = SLOTS // 2
F32 = jnp.float32
BF16 = jnp.bfloat16

NN = (((1,), (0,)), ((), ()))
NT = (((1,), (1,)), ((), ()))
TN = (((0,), (0,)), ((), ()))


def dot(a, b, dims=NN):
    return lax.dot_general(a, b, dims, preferred_element_type=F32)


def kernel_call(body, outs, cost, operands, scratch=(), vmem=48):
    specs = [pl.BlockSpec(memory_space=pltpu.SMEM if x.shape == (1,) else pltpu.VMEM) for x in operands]
    call = pl.pallas_call(
        body,
        out_shape=outs,
        in_specs=specs,
        scratch_shapes=list(scratch),
        compiler_params=pltpu.CompilerParams(vmem_limit_bytes=vmem * 1024 * 1024),
        cost_estimate=pl.CostEstimate(flops=cost, bytes_accessed=1 << 20, transcendentals=0),
    )
    return call(*operands)


def column_norm(x):
    mean = jnp.mean(x, axis=0, keepdims=True)
    centred = x - mean
    var = jnp.mean(centred * centred, axis=0, keepdims=True)
    return (centred * lax.rsqrt(var + 1e-05)).astype(BF16)


def place_blocks(dst, blocks, me):
    for k, block in enumerate(blocks):
        owner = lax.rem(me + CHAN - k, CHAN)
        size = block.shape[0]
        dst[pl.ds(pl.multiple_of(owner * size, size), size), :] = block[...]


def attention_body(me_ref, x0, x1, x2, x3, w_ref, out_ref, xs, qkv):
    place_blocks(xs, (x0, x1, x2, x3), me_ref[0])
    rows = xs.shape[1]
    norm = column_norm(xs[...].astype(F32))
    proj = dot(w_ref[...], norm)
    width = out_ref.shape[0]
    qkv[0:width, :] = (proj[0:width].astype(BF16) * BF16(0.25)).astype(BF16)
    qkv[width:, :] = proj[width:].astype(BF16)
    ones = (lax.broadcasted_iota(jnp.int32, (HD, rows), 0) == 0).astype(F32).astype(BF16)
    block = 256
    for head in range(width // HD):
        lo = head * HD
        keys = qkv[width + lo : width + lo + HD, :]
        vals = jnp.concatenate([qkv[2 * width + lo : 2 * width + lo + HD, :], ones], axis=0)
        for part in range(rows // block):
            cols = slice(part * block, (part + 1) * block)
            scores = dot(qkv[lo : lo + HD, cols], keys, TN)
            top = jnp.max(scores, axis=1, keepdims=True)
            expo = jnp.exp(scores - top).astype(BF16)
            res = dot(vals, expo, NT)
            out_ref[lo : lo + HD, cols] = (res[0:HD] / res[HD : HD + 1]).astype(BF16)


def pack_body(core_ref, conv_ref, up_ref, down_ref, out_ref):
    half = pl.ds(pl.multiple_of(core_ref[0] * 128, 128), 128)
    rows = conv_ref.shape[0]
    out_ref[0:rows, :] = conv_ref[:, half]
    size = up_ref.shape[1]
    out_ref[rows : rows + size, :] = up_ref[half, :].astype(F32).T.astype(BF16)
    out_ref[rows + size :, :] = down_ref[half, :].astype(F32).T.astype(BF16)


def code_body(rank_ref, code_ref):
    rank = rank_ref[...]
    rows = rank.shape[1]
    owner = rank // rows
    onehot = (lax.broadcasted_iota(jnp.int32, (rows // HALF, rows), 0) == owner).astype(F32)
    up_to = lax.broadcasted_iota(jnp.int32, (rows, rows), 0) <= lax.broadcasted_iota(
        jnp.int32, (rows, rows), 1
    )
    count = dot(onehot.astype(BF16), up_to.astype(F32).astype(BF16))
    slot = jnp.sum(onehot * count, axis=0, keepdims=True).astype(jnp.int32) - 1
    high = (slot >= HALF).astype(jnp.int32)
    code_ref[...] = owner * HALF + slot + high * (rows - HALF)


def slot_match(code, half, start, size, cols):
    rows = lax.broadcasted_iota(jnp.int32, (size, cols), 0) + (start + half * 1024)
    return (rows == code).astype(F32).astype(BF16)


def send_body(me_ref, range_ref, h0, h1, h2, h3, x_ref, w_ref, code_ref, rank_ref, out_ref, hs):
    place_blocks(hs, (h0, h1, h2, h3), me_ref[0])
    first = (x_ref[...].astype(F32) + dot(w_ref[...], hs[...])).astype(BF16)
    zero = jnp.zeros_like(first)
    low = jnp.concatenate([first, zero], axis=0)
    high = jnp.concatenate([zero, first], axis=0)
    code = code_ref[...]
    rows = code.shape[1]
    local = rank_ref[...] % rows
    tens = (local // 32 + 1).astype(F32)
    ones = (local % 32).astype(F32)
    line = lax.broadcasted_iota(jnp.int32, (8, rows), 0)
    low_info = jnp.where(line == 0, tens, jnp.where(line == 1, ones, 0.0)).astype(BF16)
    high_info = jnp.where(line == 2, tens, jnp.where(line == 3, ones, 0.0)).astype(BF16)
    block = 256
    at = lax.rem(range_ref[0], 8) * HALF
    lane = lax.broadcasted_iota(jnp.int32, (8, 128), 1)
    keep = (lane >= at) & (lane < at + HALF)
    for start in range(0, rows, block):
        low_match = slot_match(code, 0, start, block, rows)
        high_match = slot_match(code, 1, start, block, rows)
        res = dot(low_match, low, NT) + dot(high_match, high, NT)
        info = dot(low_info, low_match, NT) + dot(high_info, high_match, NT)
        first_owner = start // HALF
        owners = block // HALF
        out_ref[first_owner : first_owner + owners, 0:HALF, :] = res.astype(BF16).reshape(
            owners, HALF, 128
        )
        for i in range(owners):
            turned = pltpu.roll(info, lax.rem(at + block - i * HALF, block), 1)
            out_ref[first_owner + i, HALF : HALF + 8, :] = jnp.where(
                keep, turned[:, 0:128], 0.0
            ).astype(BF16)


def group_body(got_ref, core_ref, quarters_ref, near_edge, far_edge, place_ref):
    core = core_ref[0]
    width = quarters_ref.shape[1]
    owners = got_ref.shape[0]
    slots = owners * HALF
    got = got_ref[:, 0:HALF, :].reshape(slots, 2 * width).astype(F32).T.astype(BF16)
    info = got_ref[:, HALF : HALF + 8, :].astype(F32).reshape(owners // 8, 8, 8, 128)
    info = jnp.sum(info, axis=1)
    info = jnp.concatenate([info[g] for g in range(owners // 8)], axis=1)
    low_place = info[0:1] * 32.0 + info[1:2] - 32.0
    high_place = info[2:3] * 32.0 + info[3:4] - 32.0
    place_ref[...] = jnp.concatenate([low_place, high_place, jnp.zeros((6, slots), F32)], axis=0)
    for q in range(CHAN):
        rows = lax.broadcasted_iota(jnp.int32, (256, slots), 0).astype(F32) + q * 256.0
        res = 0.0
        for half, place in enumerate((low_place, high_place)):
            match = (rows == place).astype(F32).astype(BF16)
            res += dot(got[half * width : (half + 1) * width], match, NT)
        quarters_ref[q] = res.astype(BF16)

    @pl.when(core == 0)
    def _():
        near_edge[...] = quarters_ref[CHAN - 1]
        far_edge[...] = quarters_ref[0]

    @pl.when(core == 1)
    def _():
        near_edge[...] = quarters_ref[0]
        far_edge[...] = quarters_ref[CHAN - 1]


def window_body(me_ref, core_ref, quarters_ref, near_edge, far_edge, m0, m1, m2, m3, ext):
    core = core_ref[0]
    for q in range(CHAN):
        ext[q + 1] = quarters_ref[q]

    @pl.when(core == 0)
    def _():
        ext[0] = far_edge[...]
        ext[CHAN + 1] = near_edge[...]

    @pl.when(core == 1)
    def _():
        ext[0] = near_edge[...]
        ext[CHAN + 1] = far_edge[...]

    for k, ref in enumerate((m0, m1, m2, m3)):
        ref[...] = ext[pl.ds(lax.rem(me_ref[0] + k, CHAN), 3)]


def conv_body(me_ref, core_ref, *refs):
    msgs = refs[0:4]
    near_ref, near_w, far_w = refs[4:7]
    outs = refs[7:11]
    win, third_ref = refs[11:13]
    me = me_ref[0]
    core = core_ref[0]
    quarter = 64
    whole = CHAN * quarter
    shift = 2 * core

    def rotated(owner):
        return pl.ds(pl.multiple_of(lax.rem(owner + shift, CHAN) * quarter, quarter), quarter)

    def weight(block, at, size):
        rows = pl.ds(pl.multiple_of(at, quarter), size)
        return jnp.concatenate([near_w[block, rows, :], far_w[block, rows, :]], axis=1)

    def kernel(j):
        return jnp.concatenate(
            [weight(lax.rem(i + shift, CHAN), j * quarter, quarter) for i in range(CHAN)], axis=0
        )

    for k in range(CHAN):
        at = rotated(me + CHAN - k)
        for b in range(3):
            win[at, b * 256 : (b + 1) * 256] = msgs[k][b]

    near = near_ref[...]
    target = jnp.where(near < 0, -1, near + lax.broadcasted_iota(jnp.int32, near.shape, 1))
    target = jnp.concatenate([target.astype(F32), jnp.zeros((5, whole), F32)], axis=0).T
    cols = lax.broadcasted_iota(jnp.int32, (256, 768), 1).astype(F32)
    second = win[:, 256:512].astype(F32)
    group = 3
    for start in range(0, KER, group):
        match = [(cols == target[:, j : j + 1]).astype(F32).astype(BF16) for j in range(start, start + group)]
        picked = dot(jnp.concatenate(match, axis=0), win[...], NT).astype(BF16)
        picked = jnp.concatenate([picked[i * 256 : (i + 1) * 256] for i in range(group)], axis=1)
        kernels = jnp.concatenate([kernel(j) for j in range(start, start + group)], axis=1)
        second += dot(kernels, picked, NT)
    second = second.astype(BF16)
    norm = column_norm(second.astype(F32))
    total = second.astype(F32)
    half = whole // 2
    lo, hi = half * core, half * (1 - core)
    for i in range(CHAN):
        base = KER * quarter
        up = jnp.concatenate([weight(i, base + lo, half), weight(i, base + hi, half)], axis=0)
        base = base + whole
        down = jnp.concatenate([weight(i, base + lo, half), weight(i, base + hi, half)], axis=0)
        hidden = dot(up, norm)
        hidden = (0.5 * hidden * (1.0 + lax.erf(hidden * (2.0 ** -0.5)))).astype(BF16)
        total += dot(down, hidden)
    third_ref[...] = total.astype(BF16)
    for k in range(CHAN):
        outs[k][...] = third_ref[rotated(me + k), :]


def back_body(me_ref, t0, t1, t2, t3, place_ref, out_ref, tmp):
    me = me_ref[0]
    for k, ref in enumerate((t0, t1, t2, t3)):
        tmp[lax.rem(me + CHAN - k, CHAN)] = ref[...]
    third = jnp.concatenate([tmp[q] for q in range(CHAN)], axis=1)
    zero = jnp.zeros_like(third)
    low = jnp.concatenate([third, zero], axis=0)
    high = jnp.concatenate([zero, third], axis=0)
    column = place_ref[...].T
    block = 256
    rank = lax.broadcasted_iota(jnp.int32, (block, third.shape[1]), 1).astype(F32)
    for start in range(0, column.shape[0], block):
        res = 0.0
        for half, rhs in enumerate((low, high)):
            match = (rank == column[start : start + block, half : half + 1]).astype(F32).astype(BF16)
            res += dot(match, rhs, NT)
        owner = start // HALF
        out_ref[owner : owner + block // HALF] = res.astype(BF16).reshape(block // HALF, HALF, 128)


def restore_body(got_ref, code_ref, out_ref):
    width = out_ref.shape[0]
    got = got_ref[...].reshape(-1, 2 * width).astype(F32).T.astype(BF16)
    code = code_ref[...]
    res = 0.0
    for half in range(2):
        for start in range(0, got.shape[1], 256):
            match = slot_match(code, half, start, 256, code.shape[1])
            res += dot(got[half * width : (half + 1) * width, start : start + 256], match)
    out_ref[...] = res.astype(BF16)


def turn(k):
    return [(i, (i + k) % CHAN) for i in range(CHAN)]


def gather_chan(x):
    return [x] + [lax.ppermute(x, "chan", turn(k)) for k in range(1, CHAN)]


def shards(
    features, hilbert_rank, neighbours, qkv_weight, out_weight, conv_weight, up_weight, down_weight
):
    quarter, rows = features.shape
    owners = lax.axis_size("range")
    me = lax.axis_index("chan").astype(jnp.int32)
    me_ref = me[None]
    sds = jax.ShapeDtypeStruct

    with jax.named_scope("gather_features"):
        blocks = gather_chan(features)
    core = lax.rem(lax.axis_index("range").astype(jnp.int32), 2)
    core_ref = core[None]
    rank = hilbert_rank[None, :]
    with jax.named_scope("gather_weights"):
        packed = kernel_call(
            pack_body,
            sds((KER * quarter + 2 * up_weight.shape[1], 128), BF16),
            1 << 20,
            [core_ref, conv_weight.reshape(KER * quarter, -1), up_weight, down_weight],
        )
        near_w = lax.all_gather(packed, "chan", axis=0)
    with jax.named_scope("codes"):
        code = kernel_call(code_body, sds((1, rows), jnp.int32), 1 << 20, [rank])

    qkv = jnp.transpose(qkv_weight, (0, 2, 1)).reshape(3 * quarter, -1)
    with jax.named_scope("attention"):
        heads = kernel_call(
            attention_body,
            sds((quarter, rows), BF16),
            1 << 32,
            [me_ref] + blocks + [qkv],
            [pltpu.VMEM((CHAN * quarter, rows), BF16), pltpu.VMEM((3 * quarter, rows), BF16)],
        )
    with jax.named_scope("gather_heads"):
        blocks = gather_chan(heads)
    with jax.named_scope("send"):
        range_ref = lax.axis_index("range").astype(jnp.int32)[None]
        send = kernel_call(
            send_body,
            sds((owners, HALF + 8, 2 * quarter), BF16),
            1 << 30,
            [me_ref, range_ref] + blocks + [features, out_weight.T, code, rank],
            [pltpu.VMEM((CHAN * quarter, rows), BF16)],
        )
        got = exchange(send)
        near_w, got = lax.optimization_barrier((near_w, got))
        far_w = lax.ppermute(near_w, "range", [(i, i ^ 1) for i in range(owners)])
    with jax.named_scope("group"):
        part = sds((3, quarter, 256), BF16)
        edge = sds((quarter, 256), BF16)
        quarters, near_edge, far_edge, place = kernel_call(
            group_body,
            (sds((CHAN, quarter, 256), BF16), edge, edge, sds((8, rows), F32)),
            1 << 30,
            [got, core_ref],
        )
    with jax.named_scope("halo"):
        near_edge = lax.ppermute(near_edge, "range", [(i, i ^ 1) for i in range(owners)])
        pairs = [(i, i + 1) for i in range(1, owners - 1, 2)]
        far_edge = lax.ppermute(far_edge, "range", pairs + [(j, i) for i, j in pairs])
    with jax.named_scope("gather_window"):
        msgs = kernel_call(
            window_body,
            (part, part, part, part),
            1 << 20,
            [me_ref, core_ref, quarters, near_edge, far_edge],
            [pltpu.VMEM((CHAN + 2, quarter, 256), BF16)],
        )
        msgs = [msgs[0]] + [lax.ppermute(msgs[k], "chan", turn(k)) for k in range(1, CHAN)]
    with jax.named_scope("conv_mlp"):
        near = lax.dynamic_slice_in_dim(neighbours, me * 256, 256, 1)
        thirds = kernel_call(
            conv_body,
            (edge, edge, edge, edge),
            1 << 32,
            [me_ref, core_ref] + msgs + [near, near_w, far_w],
            [
                pltpu.VMEM((CHAN * quarter, 768), BF16),
                pltpu.VMEM((CHAN * quarter, 256), BF16),
            ],
        )
    with jax.named_scope("turn_back"):
        thirds = [thirds[0]] + [lax.ppermute(thirds[k], "chan", turn(k)) for k in range(1, CHAN)]
    with jax.named_scope("back"):
        back = kernel_call(
            back_body,
            sds((owners, HALF, 2 * quarter), BF16),
            1 << 30,
            [me_ref] + thirds + [place],
            [pltpu.VMEM((CHAN, quarter, 256), BF16)],
        )
        returned = exchange(back)
    with jax.named_scope("restore"):
        return kernel_call(restore_body, sds((quarter, rows), BF16), 1 << 30, [returned, code])


def exchange(parts):
    return lax.all_to_all(parts, "range", split_axis=0, concat_axis=0, tiled=True)


def solution(mesh):
    in_specs = (
        P("chan", "range"),
        P("range"),
        P(None, "range"),
        P(None, None, "chan"),
        P(None, "chan"),
        P(None, "chan", None),
        P(None, "chan"),
        P("chan", None),
    )
    out_specs = P("chan", "range")
    return jax.shard_map(shards, mesh=mesh, in_specs=in_specs, out_specs=out_specs, check_vma=False)
```

```python
import functools

import jax
import jax.numpy as jnp
from jax import lax
from jax.experimental import pallas as pl
from jax.experimental.pallas import tpu as pltpu
from jax.sharding import PartitionSpec as P

HD = 16
KER = 27
HW = 256
CHAN = 4
SLOTS = 32
TURN = SLOTS // CHAN
INFO = 16
TENS = 4
ONES = 5
F32 = jnp.float32
BF16 = jnp.bfloat16
I32 = jnp.int32

NN = (((1,), (0,)), ((), ()))
NT = (((1,), (1,)), ((), ()))
TN = (((0,), (0,)), ((), ()))


def dot(a, b, dims=NN):
    return lax.dot_general(a, b, dims, preferred_element_type=F32)


def iota(shape, axis):
    return lax.broadcasted_iota(I32, shape, axis)


def hot(mask):
    return mask.astype(F32).astype(BF16)


def kernel_call(body, outs, cost, operands, scratch=(), vmem=48, managed=False):
    place = None if managed else pltpu.VMEM
    specs = [pl.BlockSpec(memory_space=pltpu.SMEM if x.shape == (1,) else place) for x in operands]
    call = pl.pallas_call(
        body,
        out_shape=outs,
        in_specs=specs,
        scratch_shapes=list(scratch),
        compiler_params=pltpu.CompilerParams(vmem_limit_bytes=vmem * 1024 * 1024),
        cost_estimate=pl.CostEstimate(flops=cost, bytes_accessed=1 << 20, transcendentals=0),
    )
    return call(*operands)


def column_norm(x):
    mean = jnp.mean(x, axis=0, keepdims=True)
    centred = x - mean
    var = jnp.mean(centred * centred, axis=0, keepdims=True)
    return (centred * lax.rsqrt(var + 1e-05)).astype(BF16)


def sender(me, k):
    return lax.rem(me + CHAN - k, CHAN)


def code_body(owners, me_ref, rank_ref, out_ref):
    rank = rank_ref[...]
    rows = rank.shape[1]
    owner = rank // rows
    local = rank % rows
    onehot = (iota((owners, rows), 0) == owner).astype(F32)
    up_to = hot(iota((rows, rows), 0) <= iota((rows, rows), 1))
    count = dot(onehot.astype(BF16), up_to)
    below = hot(iota((owners, owners), 1) < iota((owners, owners), 0))
    start = dot(below, count[:, rows - 128 :].astype(BF16))[:, 127:128]
    begin = jnp.sum(onehot * start, axis=0, keepdims=True).astype(I32)
    place = jnp.sum(onehot * (start + count - 1.0), axis=0, keepdims=True).astype(I32)
    turn = place % CHAN
    row = place // CHAN
    slot = row - (begin - turn + CHAN - 1) // CHAN
    back = (turn // 2) * rows + owner * (2 * TURN) + (turn % 2) * TURN + slot
    mine = jnp.where(turn == me_ref[0], row, -1)
    lines = (back, mine, owner, slot, local // 32 + 1, local % 32)
    out_ref[...] = jnp.concatenate(lines + (back, back), axis=0)


def merge_body(x_ref, qkv_ref, out_w_ref, out_ref):
    quarter, rows = x_ref.shape
    whole = qkv_ref.shape[1]
    out_ref[0:quarter, :] = x_ref[...]
    for part in range(3):
        cut = slice(part * quarter, (part + 1) * quarter)
        out_ref[quarter:, part * whole : (part + 1) * whole] = qkv_ref[cut, :]
    out_ref[quarter:, 3 * whole :] = out_w_ref[...]


def attention_body(me_ref, range_ref, *refs):
    blocks = refs[0:4]
    codes_ref, send_ref, xs, ws, heads = refs[4:9]
    me = me_ref[0]
    quarter = blocks[0].shape[0] // 2
    for k in range(CHAN):
        owner = sender(me, k)
        xs[pl.ds(pl.multiple_of(owner * quarter, quarter), quarter), :] = blocks[k][0:quarter, :]
        ws[owner] = blocks[k][quarter:, :]

    codes = codes_ref[...]
    width, rows = xs.shape

    def weight(part):
        cut = slice(part * width, (part + 1) * width)
        return jnp.concatenate([ws[i, :, cut] for i in range(CHAN)], axis=0)

    mine = rows // CHAN
    x = xs[...]
    norm = column_norm(x.astype(F32))
    pick = hot(iota((mine, rows), 0) == codes[1:2])
    own = dot(x, pick, NT)
    own_norm = dot(norm, pick, NT).astype(BF16)
    digits = dot(codes.astype(F32).astype(BF16), pick, NT)
    q = (dot(weight(0), own_norm).astype(BF16) * BF16(0.25)).astype(BF16)
    keys = dot(weight(1), norm).astype(BF16)
    vals = dot(weight(2), norm).astype(BF16)
    ones = hot(iota((HD, rows), 0) == 0)
    for lo in range(0, width, HD):
        at = slice(lo, lo + HD)
        scores = dot(q[at], keys[at], TN)
        top = jnp.max(scores, axis=1, keepdims=True)
        expo = jnp.exp(scores - top).astype(BF16)
        res = dot(jnp.concatenate([vals[at], ones], axis=0), expo, NT)
        heads[at, :] = (res[0:HD] / res[HD : HD + 1]).astype(BF16)
    first = (own + dot(weight(3), heads[...])).astype(BF16)

    target = digits[2:3] * TURN + digits[3:4]
    low_digits = digits.astype(BF16)
    shift = lax.rem(range_ref[0], 128 // TURN) * TURN
    lane = iota((8, 128), 1)
    keep = (lane >= shift) & (lane < shift + TURN)
    block = 256
    owners = block // TURN
    for start in range(0, send_ref.shape[0] * TURN, block):
        match = hot((iota((block, mine), 0) + start).astype(F32) == target)
        res = dot(match, first, NT).reshape(owners, TURN, width)
        info = dot(low_digits, match, NT)
        tiles = []
        for i in range(owners):
            turned = pltpu.roll(info, lax.rem(shift + block - i * TURN, block), 1)
            tiles.append(jnp.where(keep, turned[:, 0:128], 0.0)[None])
        tiles = jnp.concatenate(tiles, axis=0)
        res = jnp.concatenate([res[:, :, 0:128], res[:, :, 128:], tiles], axis=1)
        owner = start // TURN
        send_ref[owner : owner + owners] = res.astype(BF16)


def compact_body(got_ref, out_ref):
    owners = got_ref.shape[0]
    slots = owners * TURN
    got = got_ref[...].astype(F32)
    info = got[:, 2 * TURN :, :].reshape(slots // 128, 128 // TURN, 8, 128)
    info = jnp.sum(info, axis=1)
    info = jnp.concatenate([info[g] for g in range(slots // 128)], axis=1)
    valid = info[TENS : TENS + 1] > 0.0
    before = hot(iota((slots, slots), 0) < iota((slots, slots), 1))
    line = jnp.broadcast_to(valid.astype(F32), (8, slots)).astype(BF16)
    position = jnp.where(valid, dot(line, before)[0:1], -1.0)
    match = hot(iota((slots, slots), 0).astype(F32) == position)
    rows = [got[:, i * TURN : (i + 1) * TURN, :].reshape(slots, 128) for i in range(2)]
    rows = jnp.concatenate(rows, axis=1).astype(BF16)
    limit = out_ref.shape[0] - INFO
    found = dot(match[0:limit], rows)
    packed = dot(info.astype(BF16), match, NT)
    lines = []
    for table in (packed, info):
        for digit in (TENS, ONES):
            lines += [table[digit : digit + 1, 0:256], table[digit : digit + 1, 256:]]
    lines.append(jnp.zeros((INFO - len(lines), 256), F32))
    out_ref[...] = jnp.concatenate([found] + lines, axis=0).astype(BF16)


def turned_lanes(x, core):
    half = x.shape[1] // 2
    return jnp.where(core == 1, jnp.concatenate([x[:, half:], x[:, :half]], axis=1), x)


def window_body(me_ref, core_ref, c0, c1, c2, c3, win_ref, third_ref, place_ref, stack):
    me = me_ref[0]
    for k, ref in enumerate((c0, c1, c2, c3)):
        stack[sender(me, k)] = ref[...]
    limit = stack.shape[1] - INFO
    line = iota((256, limit), 0)
    side = jnp.where(me == 0, 1, me - 1)
    other = jnp.where(me == 0, 3, jnp.where(me == 3, 0, me + 1))
    ranks = jnp.concatenate([line + me * 256, line + side * 256, line + other * 256], axis=0)
    ranks = ranks.astype(F32)
    total = 0.0
    places = []
    for i in range(CHAN):
        info = stack[i, limit:, :].astype(F32)

        def value(at):
            tens = jnp.concatenate([info[at : at + 1], info[at + 1 : at + 2]], axis=1)
            ones = jnp.concatenate([info[at + 2 : at + 3], info[at + 3 : at + 4]], axis=1)
            return tens * 32.0 + ones - 32.0

        places.append(value(4))
        total += dot(hot(ranks == value(0)[:, 0:limit]), stack[i, 0:limit, :])
    places.append(jnp.zeros_like(places[0]))
    place_ref[...] = jnp.concatenate(places + places[4:] * 3, axis=0)
    total = total.astype(BF16)
    win_ref[...] = turned_lanes(total[0:512], core_ref[0])
    third_ref[...] = total[512:]


def pack_body(core_ref, conv_ref, up_ref, down_ref, near_ref, far_ref):
    for mine, dst in ((core_ref[0], near_ref), (1 - core_ref[0], far_ref)):
        half = pl.ds(pl.multiple_of(mine * 128, 128), 128)
        at = conv_ref.shape[0]
        dst[0:at, :] = conv_ref[:, half]
        for ref in (up_ref, down_ref):
            size = ref.shape[1]
            dst[at : at + size, :] = ref[half, :].astype(F32).T.astype(BF16)
            at += size


def weight_reader(near_w, far_w, quarter):
    split = near_w[2].shape[0]

    def weight(k, section, at, size):
        if k == 2:
            piece = 2 if section < split else 3
            section = section % split
        else:
            piece = (0, 1, None, 4)[k]
        rows = pl.ds(pl.multiple_of(section + at, quarter), size)
        return jnp.concatenate([near_w[piece][rows, :], far_w[piece][rows, :]], axis=1)

    return weight


def rows_at(me, core, k, quarter):
    owner = lax.rem(me + CHAN - k + 2 * core, CHAN)
    return pl.ds(pl.multiple_of(owner * quarter, quarter), quarter)


def add_conv(total, near_ref, cols, rows, weight, quarter):
    near = near_ref[...]
    target = jnp.where(near < 0, -1, near + iota(near.shape, 1))
    target = jnp.concatenate([target.astype(F32), jnp.zeros((5, near.shape[1]), F32)], axis=0).T
    cols = cols.astype(F32)
    group = 3

    def kernel(j):
        return jnp.concatenate([weight(k, j * quarter, 0, quarter) for k in range(CHAN)], axis=0)

    for start in range(0, KER, group):
        js = range(start, start + group)
        match = jnp.concatenate([hot(cols == target[:, j : j + 1]) for j in js], axis=0)
        picked = dot(match, rows).astype(BF16)
        picked = jnp.concatenate([picked[i * 256 : (i + 1) * 256] for i in range(group)], axis=1)
        total += dot(jnp.concatenate([kernel(j) for j in js], axis=1), picked, NT)
    return total


def conv_first_body(me_ref, core_ref, win_ref, near_ref, *refs):
    near_w, far_w, out_ref, turned = refs[0:5], refs[5:10], refs[10], refs[11]
    me, core = me_ref[0], core_ref[0]
    quarter = 64
    turned[...] = win_ref[0:256, :].astype(F32).T
    own = [turned[rows_at(me, core, k, quarter), :] for k in range(CHAN)]
    lane = iota((256, 512), 1)
    cols = jnp.where(lane < 256, lane + 256, jnp.where(me == 0, lane + 256, lane - 256))
    weight = weight_reader(near_w, far_w, quarter)
    out_ref[...] = add_conv(
        jnp.concatenate(own, axis=0), near_ref, cols, win_ref[...], weight, quarter
    )


def conv_second_body(me_ref, core_ref, acc_ref, halo_ref, third_ref, near_ref, *refs):
    near_w, far_w, outs, norm_ref = refs[0:5], refs[5:10], refs[10:14], refs[14]
    me, core = me_ref[0], core_ref[0]
    quarter = 64
    whole = CHAN * quarter
    half = whole // 2
    weight = weight_reader(near_w, far_w, quarter)
    edge = (me == 0) | (me == CHAN - 1)
    rows = turned_lanes(jnp.where(edge, halo_ref[...], third_ref[...]), core)
    cols = iota((256, 256), 1) + jnp.where(me == 0, 0, 512)
    second = add_conv(acc_ref[...], near_ref, cols, rows, weight, quarter).astype(BF16)
    norm = column_norm(second.astype(F32))
    for k in range(CHAN):
        norm_ref[rows_at(me, core, k, quarter), :] = norm[k * quarter : (k + 1) * quarter]
    total = second.astype(F32)
    lo, hi = half * core, half * (1 - core)
    up_at = KER * quarter
    down_at = up_at + whole
    for k in range(CHAN):
        up = [weight(k, up_at, x, half) for x in (lo, hi)]
        hidden = dot(jnp.concatenate(up, axis=0), norm_ref[...])
        hidden = (0.5 * hidden * (1.0 + lax.erf(hidden * (2.0 ** -0.5)))).astype(BF16)
        down = [weight(k, down_at, sender(me, p) * quarter, quarter) for p in range(CHAN)]
        total += dot(jnp.concatenate(down, axis=0), hidden)
    third = total.astype(BF16)
    for k in range(CHAN):
        p = (CHAN - k) % CHAN
        outs[k][...] = third[p * quarter : (p + 1) * quarter]


def back_body(me_ref, t0, t1, t2, t3, place_ref, out_ref, tmp):
    me = me_ref[0]
    for k, ref in enumerate((t0, t1, t2, t3)):
        tmp[sender(me, k)] = ref[...]
    third = jnp.concatenate([tmp[q] for q in range(CHAN)], axis=1)
    zero = jnp.zeros_like(third)
    low = jnp.concatenate([third, zero], axis=0)
    high = jnp.concatenate([zero, third], axis=0)
    column = place_ref[...].T
    slots = column.shape[0]
    block = 256
    rank = iota((block, third.shape[1]), 1).astype(F32)
    for start in range(0, slots, block):
        res = []
        for odd in range(2):
            part = 0.0
            for half, rhs in enumerate((low, high)):
                i = 2 * half + odd
                part += dot(hot(rank == column[start : start + block, i : i + 1]), rhs, NT)
            res.append(part.reshape(block // TURN, TURN, 128))
        owner = start // TURN
        out_ref[owner : owner + block // TURN] = jnp.concatenate(res, axis=1).astype(BF16)


def restore_body(got_ref, codes_ref, out_ref):
    width, rows = out_ref.shape
    got = got_ref[...].reshape(-1, 2 * width).astype(F32).T.astype(BF16)
    code = codes_ref[0:1, :]
    res = 0.0
    for half in range(2):
        for start in range(0, got.shape[1], 256):
            match = hot(iota((256, rows), 0) + (start + half * rows) == code)
            res += dot(got[half * width : (half + 1) * width, start : start + 256], match)
    out_ref[...] = res.astype(BF16)


def turn(k):
    return [(i, (i + k) % CHAN) for i in range(CHAN)]


def gather_chan(x):
    return [x] + [lax.ppermute(x, "chan", turn(k)) for k in range(1, CHAN)]


def exchange(parts):
    return lax.all_to_all(parts, "range", split_axis=0, concat_axis=0, tiled=True)


def shards(
    features, hilbert_rank, neighbours, qkv_weight, out_weight, conv_weight, up_weight, down_weight
):
    quarter, rows = features.shape
    whole = CHAN * quarter
    owners = lax.axis_size("range")
    me = lax.axis_index("chan").astype(I32)
    position = lax.axis_index("range").astype(I32)
    core = lax.rem(position, 2)
    me_ref, core_ref, range_ref = me[None], core[None], position[None]
    swap = [(i, i ^ 1) for i in range(owners)]
    sds = jax.ShapeDtypeStruct
    vmem = pltpu.VMEM

    with jax.named_scope("gather_features"):
        qkv = jnp.transpose(qkv_weight, (0, 2, 1)).reshape(3 * quarter, whole)
        merged = kernel_call(
            merge_body,
            sds((2 * quarter, rows), BF16),
            1 << 20,
            [features, qkv, out_weight.T],
            managed=True,
        )
        blocks = gather_chan(merged)
    with jax.named_scope("codes"):
        codes = kernel_call(
            functools.partial(code_body, owners),
            sds((8, rows), I32),
            1 << 20,
            [me_ref, hilbert_rank[None, :]],
            managed=True,
        )
    with jax.named_scope("gather_weights"):
        size = KER * quarter + 2 * up_weight.shape[1]
        split = (size // quarter + 1) // 2 * quarter
        near0, far0 = kernel_call(
            pack_body,
            (sds((size, 128), BF16), sds((size, 128), BF16)),
            1 << 20,
            [core_ref, conv_weight.reshape(KER * quarter, whole), up_weight, down_weight],
            managed=True,
        )
        blocks, codes, near0, far0 = lax.optimization_barrier((blocks, codes, near0, far0))
        near1 = lax.ppermute(near0, "chan", turn(1))
        near3 = lax.ppermute(near0, "chan", turn(3))
    with jax.named_scope("attention"):
        send = kernel_call(
            attention_body,
            sds((owners, 3 * TURN, 128), BF16),
            1 << 32,
            [me_ref, range_ref] + blocks + [codes],
            [
                vmem((whole, rows), BF16),
                vmem((CHAN, quarter, rows), BF16),
                vmem((whole, rows // CHAN), BF16),
            ],
        )
    with jax.named_scope("exchange"):
        send, near1, near3 = lax.optimization_barrier((send, near1, near3))
        near2 = (
            lax.ppermute(near1[:split], "chan", turn(1)),
            lax.ppermute(near3[split:], "chan", turn(3)),
        )
        got = exchange(send)
        got, near2 = lax.optimization_barrier((got, near2))
        near_w = [near0, near1, near2[0], near2[1], near3]
        far_w = [far0] + [lax.ppermute(w, "range", swap) for w in near_w[1:]]
    with jax.named_scope("compact"):
        limit = (rows + (CHAN - 1) * owners) // CHAN
        limit = (limit + 15) // 16 * 16
        found = kernel_call(compact_body, sds((limit + INFO, whole), BF16), 1 << 28, [got])
        found = gather_chan(found)
        found, far_w = lax.optimization_barrier((found, far_w))
    with jax.named_scope("window"):
        win, third, place = kernel_call(
            window_body,
            (sds((512, whole), BF16), sds((256, whole), BF16), sds((8, owners * TURN), F32)),
            1 << 28,
            [me_ref, core_ref] + found,
            [vmem((CHAN, limit + INFO, whole), BF16)],
        )
        pairs = [(i * CHAN, (i + 1) * CHAN) for i in range(owners - 1)]
        pairs += [((i + 1) * CHAN + CHAN - 1, i * CHAN + CHAN - 1) for i in range(owners - 1)]
        halo = lax.ppermute(third, ("range", "chan"), pairs)
    with jax.named_scope("conv"):
        near_ranks = lax.dynamic_slice_in_dim(neighbours, me * 256, 256, 1)
        acc = kernel_call(
            conv_first_body,
            sds((whole, 256), F32),
            1 << 32,
            [me_ref, core_ref, win, near_ranks] + near_w + far_w,
            [vmem((whole, 256), F32)],
        )
        edge = sds((quarter, 256), BF16)
        thirds = kernel_call(
            conv_second_body,
            (edge, edge, edge, edge),
            1 << 32,
            [me_ref, core_ref, acc, halo, third, near_ranks] + near_w + far_w,
            [vmem((whole, 256), BF16)],
        )
    with jax.named_scope("turn_back"):
        thirds = [thirds[0]] + [lax.ppermute(thirds[k], "chan", turn(k)) for k in range(1, CHAN)]
    with jax.named_scope("back"):
        back = kernel_call(
            back_body,
            sds((owners, 2 * TURN, 128), BF16),
            1 << 30,
            [me_ref] + thirds + [place],
            [vmem((CHAN, quarter, 256), BF16)],
        )
        returned = exchange(back)
    with jax.named_scope("restore"):
        return kernel_call(restore_body, sds((quarter, rows), BF16), 1 << 30, [returned, codes])


def solution(mesh):
    in_specs = (
        P("chan", "range"),
        P("range"),
        P(None, "range"),
        P(None, None, "chan"),
        P(None, "chan"),
        P(None, "chan", None),
        P(None, "chan"),
        P("chan", None),
    )
    out_specs = P("chan", "range")
    return jax.shard_map(shards, mesh=mesh, in_specs=in_specs, out_specs=out_specs, check_vma=False)
```

```python
import functools

import jax
import jax.numpy as jnp
from jax import lax
from jax.experimental import pallas as pl
from jax.experimental.pallas import tpu as pltpu
from jax.sharding import PartitionSpec as P

HD = 16
KER = 27
HW = 256
CHAN = 4
SLOTS = 32
TURN = SLOTS // CHAN
INFO = 16
TENS = 4
ONES = 5
F32 = jnp.float32
BF16 = jnp.bfloat16
I32 = jnp.int32

NN = (((1,), (0,)), ((), ()))
NT = (((1,), (1,)), ((), ()))
TN = (((0,), (0,)), ((), ()))


def dot(a, b, dims=NN):
    return lax.dot_general(a, b, dims, preferred_element_type=F32)


def iota(shape, axis):
    return lax.broadcasted_iota(I32, shape, axis)


def hot(mask):
    return mask.astype(F32).astype(BF16)


def kernel_call(body, outs, cost, operands, scratch=(), vmem=24, managed=False):
    place = None if managed else pltpu.VMEM
    vmem = 62 if managed else vmem
    specs = [pl.BlockSpec(memory_space=pltpu.SMEM if x.shape == (1,) else place) for x in operands]
    call = pl.pallas_call(
        body,
        out_shape=outs,
        in_specs=specs,
        scratch_shapes=list(scratch),
        compiler_params=pltpu.CompilerParams(vmem_limit_bytes=vmem * 1024 * 1024),
        cost_estimate=pl.CostEstimate(flops=cost, bytes_accessed=1 << 20, transcendentals=0),
    )
    return call(*operands)


def column_norm(x):
    mean = jnp.mean(x, axis=0, keepdims=True)
    centred = x - mean
    var = jnp.mean(centred * centred, axis=0, keepdims=True)
    return (centred * lax.rsqrt(var + 1e-05)).astype(BF16)


def sender(me, k):
    return lax.rem(me + CHAN - k, CHAN)


def code_body(owners, me_ref, rank_ref, out_ref):
    rank = rank_ref[...]
    rows = rank.shape[1]
    owner = rank // rows
    local = rank % rows
    onehot = (iota((owners, rows), 0) == owner).astype(F32)
    up_to = hot(iota((rows, rows), 0) <= iota((rows, rows), 1))
    count = dot(onehot.astype(BF16), up_to)
    below = hot(iota((owners, owners), 1) < iota((owners, owners), 0))
    start = dot(below, count[:, rows - 128 :].astype(BF16))[:, 127:128]
    begin = jnp.sum(onehot * start, axis=0, keepdims=True).astype(I32)
    place = jnp.sum(onehot * (start + count - 1.0), axis=0, keepdims=True).astype(I32)
    turn = place % CHAN
    row = place // CHAN
    slot = row - (begin - turn + CHAN - 1) // CHAN
    back = (turn // 2) * rows + owner * (2 * TURN) + (turn % 2) * TURN + slot
    mine = jnp.where(turn == me_ref[0], row, -1)
    lines = (back, mine, owner, slot, local // 32 + 1, local % 32)
    out_ref[...] = jnp.concatenate(lines + (back, back), axis=0)


def merge_body(x_ref, qkv_ref, out_w_ref, out_ref):
    quarter, rows = x_ref.shape
    whole = qkv_ref.shape[1]
    out_ref[0:quarter, :] = x_ref[...]
    for part in range(3):
        cut = slice(part * quarter, (part + 1) * quarter)
        out_ref[quarter:, part * whole : (part + 1) * whole] = qkv_ref[cut, :]
    out_ref[quarter:, 3 * whole :] = out_w_ref[...]


def attention_body(me_ref, range_ref, *refs):
    blocks = refs[0:4]
    codes_ref, send_ref, xs, ws, heads = refs[4:9]
    me = me_ref[0]
    quarter = blocks[0].shape[0] // 2
    for k in range(CHAN):
        owner = sender(me, k)
        xs[pl.ds(pl.multiple_of(owner * quarter, quarter), quarter), :] = blocks[k][0:quarter, :]
        ws[owner] = blocks[k][quarter:, :]

    codes = codes_ref[...]
    width, rows = xs.shape

    def weight(part):
        cut = slice(part * width, (part + 1) * width)
        return jnp.concatenate([ws[i, :, cut] for i in range(CHAN)], axis=0)

    mine = rows // CHAN
    x = xs[...]
    norm = column_norm(x.astype(F32))
    pick = hot(iota((mine, rows), 0) == codes[1:2])
    own = dot(x, pick, NT)
    own_norm = dot(norm, pick, NT).astype(BF16)
    digits = dot(codes.astype(F32).astype(BF16), pick, NT)
    q = (dot(weight(0), own_norm).astype(BF16) * BF16(0.25)).astype(BF16)
    keys = dot(weight(1), norm).astype(BF16)
    vals = dot(weight(2), norm).astype(BF16)
    ones = hot(iota((HD, rows), 0) == 0)
    for lo in range(0, width, HD):
        at = slice(lo, lo + HD)
        scores = dot(q[at], keys[at], TN)
        top = jnp.max(scores, axis=1, keepdims=True)
        expo = jnp.exp(scores - top).astype(BF16)
        res = dot(jnp.concatenate([vals[at], ones], axis=0), expo, NT)
        heads[at, :] = (res[0:HD] / res[HD : HD + 1]).astype(BF16)
    first = (own + dot(weight(3), heads[...])).astype(BF16)

    target = digits[2:3] * TURN + digits[3:4]
    low_digits = digits.astype(BF16)
    shift = lax.rem(range_ref[0], 128 // TURN) * TURN
    lane = iota((8, 128), 1)
    keep = (lane >= shift) & (lane < shift + TURN)
    block = 256
    owners = block // TURN
    for start in range(0, send_ref.shape[0] * TURN, block):
        match = hot((iota((block, mine), 0) + start).astype(F32) == target)
        res = dot(match, first, NT).reshape(owners, TURN, width)
        info = dot(low_digits, match, NT)
        tiles = []
        for i in range(owners):
            turned = pltpu.roll(info, lax.rem(shift + block - i * TURN, block), 1)
            tiles.append(jnp.where(keep, turned[:, 0:128], 0.0)[None])
        tiles = jnp.concatenate(tiles, axis=0)
        res = jnp.concatenate([res[:, :, 0:128], res[:, :, 128:], tiles], axis=1)
        owner = start // TURN
        send_ref[owner : owner + owners] = res.astype(BF16)


def compact_body(got_ref, out_ref):
    owners = got_ref.shape[0]
    slots = owners * TURN
    got = got_ref[...].astype(F32)
    info = got[:, 2 * TURN :, :].reshape(slots // 128, 128 // TURN, 8, 128)
    info = jnp.sum(info, axis=1)
    info = jnp.concatenate([info[g] for g in range(slots // 128)], axis=1)
    valid = info[TENS : TENS + 1] > 0.0
    before = hot(iota((slots, slots), 0) < iota((slots, slots), 1))
    line = jnp.broadcast_to(valid.astype(F32), (8, slots)).astype(BF16)
    position = jnp.where(valid, dot(line, before)[0:1], -1.0)
    match = hot(iota((slots, slots), 0).astype(F32) == position)
    rows = [got[:, i * TURN : (i + 1) * TURN, :].reshape(slots, 128) for i in range(2)]
    rows = jnp.concatenate(rows, axis=1).astype(BF16)
    limit = out_ref.shape[0] - INFO
    found = dot(match[0:limit], rows)
    packed = dot(info.astype(BF16), match, NT)
    lines = []
    for table in (packed, info):
        for digit in (TENS, ONES):
            lines += [table[digit : digit + 1, 0:256], table[digit : digit + 1, 256:]]
    lines.append(jnp.zeros((INFO - len(lines), 256), F32))
    out_ref[...] = jnp.concatenate([found] + lines, axis=0).astype(BF16)


def turned_lanes(x, core):
    half = x.shape[1] // 2
    return jnp.where(core == 1, jnp.concatenate([x[:, half:], x[:, :half]], axis=1), x)


def window_body(me_ref, core_ref, c0, c1, c2, c3, win_ref, third_ref, place_ref, stack):
    me = me_ref[0]
    for k, ref in enumerate((c0, c1, c2, c3)):
        stack[sender(me, k)] = ref[...]
    limit = stack.shape[1] - INFO
    line = iota((256, limit), 0)
    side = jnp.where(me == 0, 1, me - 1)
    other = jnp.where(me == 0, 3, jnp.where(me == 3, 0, me + 1))
    ranks = jnp.concatenate([line + me * 256, line + side * 256, line + other * 256], axis=0)
    ranks = ranks.astype(F32)
    total = 0.0
    places = []
    for i in range(CHAN):
        info = stack[i, limit:, :].astype(F32)

        def value(at):
            tens = jnp.concatenate([info[at : at + 1], info[at + 1 : at + 2]], axis=1)
            ones = jnp.concatenate([info[at + 2 : at + 3], info[at + 3 : at + 4]], axis=1)
            return tens * 32.0 + ones - 32.0

        places.append(value(4))
        total += dot(hot(ranks == value(0)[:, 0:limit]), stack[i, 0:limit, :])
    places.append(jnp.zeros_like(places[0]))
    place_ref[...] = jnp.concatenate(places + places[4:] * 3, axis=0)
    total = total.astype(BF16)
    win_ref[...] = turned_lanes(total[0:512], core_ref[0])
    third_ref[...] = total[512:]


def pack_body(core_ref, conv_ref, up_ref, down_ref, near_ref, far_ref):
    for mine, dst in ((core_ref[0], near_ref), (1 - core_ref[0], far_ref)):
        half = pl.ds(pl.multiple_of(mine * 128, 128), 128)
        at = conv_ref.shape[0]
        dst[0:at, :] = conv_ref[:, half]
        for ref in (up_ref, down_ref):
            size = ref.shape[1]
            dst[at : at + size, :] = ref[half, :].astype(F32).T.astype(BF16)
            at += size


def weight_reader(near_w, far_w, quarter):
    def weight(k, at, size):
        rows = pl.ds(pl.multiple_of(at, quarter), size)
        return jnp.concatenate([near_w[k][rows, :], far_w[k][rows, :]], axis=1)

    return weight


def rows_at(me, core, k, quarter):
    owner = lax.rem(me + CHAN - k + 2 * core, CHAN)
    return pl.ds(pl.multiple_of(owner * quarter, quarter), quarter)


def add_conv(total, near_ref, cols, rows, weight, quarter):
    near = near_ref[...]
    target = jnp.where(near < 0, -1, near + iota(near.shape, 1))
    target = jnp.concatenate([target.astype(F32), jnp.zeros((5, near.shape[1]), F32)], axis=0).T
    cols = cols.astype(F32)
    group = 3

    def kernel(j):
        return jnp.concatenate([weight(k, j * quarter, quarter) for k in range(CHAN)], axis=0)

    for start in range(0, KER, group):
        js = range(start, start + group)
        match = jnp.concatenate([hot(cols == target[:, j : j + 1]) for j in js], axis=0)
        picked = dot(match, rows).astype(BF16)
        picked = jnp.concatenate([picked[i * 256 : (i + 1) * 256] for i in range(group)], axis=1)
        total += dot(jnp.concatenate([kernel(j) for j in js], axis=1), picked, NT)
    return total


def conv_first_body(me_ref, core_ref, win_ref, near_ref, *refs):
    near_w, far_w, out_ref, turned = refs[0:4], refs[4:8], refs[8], refs[9]
    me, core = me_ref[0], core_ref[0]
    quarter = 64
    turned[...] = win_ref[0:256, :].astype(F32).T
    own = [turned[rows_at(me, core, k, quarter), :] for k in range(CHAN)]
    lane = iota((256, 512), 1)
    cols = jnp.where(lane < 256, lane + 256, jnp.where(me == 0, lane + 256, lane - 256))
    weight = weight_reader(near_w, far_w, quarter)
    out_ref[...] = add_conv(
        jnp.concatenate(own, axis=0), near_ref, cols, win_ref[...], weight, quarter
    )


def conv_second_body(me_ref, core_ref, acc_ref, halo_ref, third_ref, near_ref, *refs):
    near_w, far_w, outs, norm_ref = refs[0:4], refs[4:8], refs[8:12], refs[12]
    me, core = me_ref[0], core_ref[0]
    quarter = 64
    whole = CHAN * quarter
    half = whole // 2
    weight = weight_reader(near_w, far_w, quarter)
    edge = (me == 0) | (me == CHAN - 1)
    rows = turned_lanes(jnp.where(edge, halo_ref[...], third_ref[...]), core)
    cols = iota((256, 256), 1) + jnp.where(me == 0, 0, 512)
    second = add_conv(acc_ref[...], near_ref, cols, rows, weight, quarter).astype(BF16)
    norm = column_norm(second.astype(F32))
    for k in range(CHAN):
        norm_ref[rows_at(me, core, k, quarter), :] = norm[k * quarter : (k + 1) * quarter]
    total = second.astype(F32)
    lo, hi = half * core, half * (1 - core)
    up_at = KER * quarter
    down_at = up_at + whole
    for k in range(CHAN):
        up = [weight(k, up_at + x, half) for x in (lo, hi)]
        hidden = dot(jnp.concatenate(up, axis=0), norm_ref[...])
        hidden = (0.5 * hidden * (1.0 + lax.erf(hidden * (2.0 ** -0.5)))).astype(BF16)
        down = [weight(k, down_at + sender(me, p) * quarter, quarter) for p in range(CHAN)]
        total += dot(jnp.concatenate(down, axis=0), hidden)
    third = total.astype(BF16)
    for k in range(CHAN):
        p = (CHAN - k) % CHAN
        outs[k][...] = third[p * quarter : (p + 1) * quarter]


def back_body(me_ref, t0, t1, t2, t3, place_ref, out_ref, tmp):
    me = me_ref[0]
    for k, ref in enumerate((t0, t1, t2, t3)):
        tmp[sender(me, k)] = ref[...]
    third = jnp.concatenate([tmp[q] for q in range(CHAN)], axis=1)
    zero = jnp.zeros_like(third)
    low = jnp.concatenate([third, zero], axis=0)
    high = jnp.concatenate([zero, third], axis=0)
    column = place_ref[...].T
    slots = column.shape[0]
    block = 256
    rank = iota((block, third.shape[1]), 1).astype(F32)
    for start in range(0, slots, block):
        res = []
        for odd in range(2):
            part = 0.0
            for half, rhs in enumerate((low, high)):
                i = 2 * half + odd
                part += dot(hot(rank == column[start : start + block, i : i + 1]), rhs, NT)
            res.append(part.reshape(block // TURN, TURN, 128))
        owner = start // TURN
        out_ref[owner : owner + block // TURN] = jnp.concatenate(res, axis=1).astype(BF16)


def restore_body(got_ref, codes_ref, out_ref):
    width, rows = out_ref.shape
    got = got_ref[...].reshape(-1, 2 * width).astype(F32).T.astype(BF16)
    code = codes_ref[0:1, :]
    res = 0.0
    for half in range(2):
        for start in range(0, got.shape[1], 256):
            match = hot(iota((256, rows), 0) + (start + half * rows) == code)
            res += dot(got[half * width : (half + 1) * width, start : start + 256], match)
    out_ref[...] = res.astype(BF16)


def turn(k):
    return [(i, (i + k) % CHAN) for i in range(CHAN)]


def gather_chan(x):
    return [x] + [lax.ppermute(x, "chan", turn(k)) for k in range(1, CHAN)]


def exchange(parts):
    return lax.all_to_all(parts, "range", split_axis=0, concat_axis=0, tiled=True)


def shards(
    features, hilbert_rank, neighbours, qkv_weight, out_weight, conv_weight, up_weight, down_weight
):
    quarter, rows = features.shape
    whole = CHAN * quarter
    owners = lax.axis_size("range")
    me = lax.axis_index("chan").astype(I32)
    position = lax.axis_index("range").astype(I32)
    core = lax.rem(position, 2)
    me_ref, core_ref, range_ref = me[None], core[None], position[None]
    swap = [(i, i ^ 1) for i in range(owners)]
    sds = jax.ShapeDtypeStruct
    vmem = pltpu.VMEM

    with jax.named_scope("gather_features"):
        qkv = jnp.transpose(qkv_weight, (0, 2, 1)).reshape(3 * quarter, whole)
        merged = kernel_call(
            merge_body,
            sds((2 * quarter, rows), BF16),
            1 << 20,
            [features, qkv, out_weight.T],
            managed=True,
        )
        blocks = gather_chan(merged)
    with jax.named_scope("codes"):
        codes = kernel_call(
            functools.partial(code_body, owners),
            sds((8, rows), I32),
            1 << 20,
            [me_ref, hilbert_rank[None, :]],
        )
    with jax.named_scope("gather_weights"):
        size = KER * quarter + 2 * up_weight.shape[1]
        near0, far0 = kernel_call(
            pack_body,
            (sds((size, 128), BF16), sds((size, 128), BF16)),
            1 << 20,
            [core_ref, conv_weight.reshape(KER * quarter, whole), up_weight, down_weight],
        )
        blocks, codes, near0, far0 = lax.optimization_barrier((blocks, codes, near0, far0))
        near_w = gather_chan(near0)
        far_w = [far0] + [lax.ppermute(w, "range", swap) for w in near_w[1:]]
    with jax.named_scope("attention"):
        send = kernel_call(
            attention_body,
            sds((owners, 3 * TURN, 128), BF16),
            1 << 32,
            [me_ref, range_ref] + blocks + [codes],
            [
                vmem((whole, rows), BF16),
                vmem((CHAN, quarter, rows), BF16),
                vmem((whole, rows // CHAN), BF16),
            ],
        )
    with jax.named_scope("exchange"):
        got = exchange(send)
        got, far_w = lax.optimization_barrier((got, far_w))
    with jax.named_scope("compact"):
        limit = (rows + (CHAN - 1) * owners) // CHAN
        limit = (limit + 15) // 16 * 16
        found = kernel_call(compact_body, sds((limit + INFO, whole), BF16), 1 << 28, [got])
        found = gather_chan(found)
        found, far_w = lax.optimization_barrier((found, far_w))
    with jax.named_scope("window"):
        win, third, place = kernel_call(
            window_body,
            (sds((512, whole), BF16), sds((256, whole), BF16), sds((8, owners * TURN), F32)),
            1 << 28,
            [me_ref, core_ref] + found,
            [vmem((CHAN, limit + INFO, whole), BF16)],
        )
        pairs = [(i * CHAN, (i + 1) * CHAN) for i in range(owners - 1)]
        pairs += [((i + 1) * CHAN + CHAN - 1, i * CHAN + CHAN - 1) for i in range(owners - 1)]
        halo = lax.ppermute(third, ("range", "chan"), pairs)
    with jax.named_scope("conv"):
        near_ranks = lax.dynamic_slice_in_dim(neighbours, me * 256, 256, 1)
        acc = kernel_call(
            conv_first_body,
            sds((whole, 256), F32),
            1 << 32,
            [me_ref, core_ref, win, near_ranks] + near_w + far_w,
            [vmem((whole, 256), F32)],
        )
        edge = sds((quarter, 256), BF16)
        thirds = kernel_call(
            conv_second_body,
            (edge, edge, edge, edge),
            1 << 32,
            [me_ref, core_ref, acc, halo, third, near_ranks] + near_w + far_w,
            [vmem((whole, 256), BF16)],
        )
    with jax.named_scope("turn_back"):
        thirds = [thirds[0]] + [lax.ppermute(thirds[k], "chan", turn(k)) for k in range(1, CHAN)]
    with jax.named_scope("back"):
        back = kernel_call(
            back_body,
            sds((owners, 2 * TURN, 128), BF16),
            1 << 30,
            [me_ref] + thirds + [place],
            [vmem((CHAN, quarter, 256), BF16)],
        )
        returned = exchange(back)
    with jax.named_scope("restore"):
        return kernel_call(restore_body, sds((quarter, rows), BF16), 1 << 30, [returned, codes])


def solution(mesh):
    in_specs = (
        P("chan", "range"),
        P("range"),
        P(None, "range"),
        P(None, None, "chan"),
        P(None, "chan"),
        P(None, "chan", None),
        P(None, "chan"),
        P("chan", None),
    )
    out_specs = P("chan", "range")
    return jax.shard_map(shards, mesh=mesh, in_specs=in_specs, out_specs=out_specs, check_vma=False)
```

```python
import functools

import jax
import jax.numpy as jnp
from jax import lax
from jax.experimental import pallas as pl
from jax.experimental.pallas import tpu as pltpu
from jax.sharding import PartitionSpec as P

HD = 16
KER = 27
HW = 256
CHAN = 4
SLOTS = 32
TURN = SLOTS // CHAN
INFO = 16
TENS = 4
ONES = 5
F32 = jnp.float32
BF16 = jnp.bfloat16
I32 = jnp.int32

NN = (((1,), (0,)), ((), ()))
NT = (((1,), (1,)), ((), ()))
TN = (((0,), (0,)), ((), ()))


def dot(a, b, dims=NN):
    return lax.dot_general(a, b, dims, preferred_element_type=F32)


def iota(shape, axis):
    return lax.broadcasted_iota(I32, shape, axis)


def hot(mask):
    return mask.astype(F32).astype(BF16)


def kernel_call(body, outs, cost, operands, scratch=(), vmem=24, managed=False):
    place = None if managed else pltpu.VMEM
    vmem = 62 if managed else vmem
    specs = [pl.BlockSpec(memory_space=pltpu.SMEM if x.shape == (1,) else place) for x in operands]
    call = pl.pallas_call(
        body,
        out_shape=outs,
        in_specs=specs,
        scratch_shapes=list(scratch),
        compiler_params=pltpu.CompilerParams(vmem_limit_bytes=vmem * 1024 * 1024),
        cost_estimate=pl.CostEstimate(flops=cost, bytes_accessed=1 << 20, transcendentals=0),
    )
    return call(*operands)


def column_norm(x):
    mean = jnp.mean(x, axis=0, keepdims=True)
    centred = x - mean
    var = jnp.mean(centred * centred, axis=0, keepdims=True)
    return (centred * lax.rsqrt(var + 1e-05)).astype(BF16)


def sender(me, k):
    return lax.rem(me + CHAN - k, CHAN)


def code_body(owners, me_ref, rank_ref, out_ref):
    rank = rank_ref[...]
    rows = rank.shape[1]
    owner = rank // rows
    local = rank % rows
    onehot = (iota((owners, rows), 0) == owner).astype(F32)
    up_to = hot(iota((rows, rows), 0) <= iota((rows, rows), 1))
    count = dot(onehot.astype(BF16), up_to)
    below = hot(iota((owners, owners), 1) < iota((owners, owners), 0))
    start = dot(below, count[:, rows - 128 :].astype(BF16))[:, 127:128]
    begin = jnp.sum(onehot * start, axis=0, keepdims=True).astype(I32)
    place = jnp.sum(onehot * (start + count - 1.0), axis=0, keepdims=True).astype(I32)
    turn = place % CHAN
    row = place // CHAN
    slot = row - (begin - turn + CHAN - 1) // CHAN
    back = (turn // 2) * rows + owner * (2 * TURN) + (turn % 2) * TURN + slot
    mine = jnp.where(turn == me_ref[0], row, -1)
    lines = (back, mine, owner, slot, local // 32 + 1, local % 32)
    out_ref[...] = jnp.concatenate(lines + (back, back), axis=0)


def merge_body(x_ref, qkv_ref, out_w_ref, out_ref):
    quarter, rows = x_ref.shape
    whole = qkv_ref.shape[1]
    out_ref[0:quarter, :] = x_ref[...]
    for part in range(3):
        cut = slice(part * quarter, (part + 1) * quarter)
        out_ref[quarter:, part * whole : (part + 1) * whole] = qkv_ref[cut, :]
    out_ref[quarter:, 3 * whole :] = out_w_ref[...]


def attention_body(me_ref, range_ref, *refs):
    blocks = refs[0:4]
    codes_ref, send_ref, xs, ws, heads = refs[4:9]
    me = me_ref[0]
    quarter = blocks[0].shape[0] // 2
    for k in range(CHAN):
        owner = sender(me, k)
        xs[pl.ds(pl.multiple_of(owner * quarter, quarter), quarter), :] = blocks[k][0:quarter, :]
        ws[owner] = blocks[k][quarter:, :]

    codes = codes_ref[...]
    width, rows = xs.shape

    def weight(part):
        cut = slice(part * width, (part + 1) * width)
        return jnp.concatenate([ws[i, :, cut] for i in range(CHAN)], axis=0)

    mine = rows // CHAN
    x = xs[...]
    norm = column_norm(x.astype(F32))
    pick = hot(iota((mine, rows), 0) == codes[1:2])
    own = dot(x, pick, NT)
    own_norm = dot(norm, pick, NT).astype(BF16)
    digits = dot(codes.astype(F32).astype(BF16), pick, NT)
    q = (dot(weight(0), own_norm).astype(BF16) * BF16(0.25)).astype(BF16)
    keys = dot(weight(1), norm).astype(BF16)
    vals = dot(weight(2), norm).astype(BF16)
    ones = hot(iota((HD, rows), 0) == 0)

    def scored(lo):
        at = slice(lo, lo + HD)
        scores = dot(q[at], keys[at], TN)
        return scores, jnp.max(scores, axis=1, keepdims=True)

    scores, top = scored(0)
    for lo in range(0, width, HD):
        later = scored(lo + HD) if lo + HD < width else (None, None)
        at = slice(lo, lo + HD)
        expo = jnp.exp(scores - top).astype(BF16)
        res = dot(jnp.concatenate([vals[at], ones], axis=0), expo, NT)
        heads[at, :] = (res[0:HD] / res[HD : HD + 1]).astype(BF16)
        scores, top = later
    first = (own + dot(weight(3), heads[...])).astype(BF16)

    target = digits[2:3] * TURN + digits[3:4]
    low_digits = digits.astype(BF16)
    shift = lax.rem(range_ref[0], 128 // TURN) * TURN
    lane = iota((8, 128), 1)
    keep = (lane >= shift) & (lane < shift + TURN)
    block = 256
    owners = block // TURN
    for start in range(0, send_ref.shape[0] * TURN, block):
        match = hot((iota((block, mine), 0) + start).astype(F32) == target)
        res = dot(match, first, NT).reshape(owners, TURN, width)
        info = dot(low_digits, match, NT)
        tiles = []
        for i in range(owners):
            turned = pltpu.roll(info, lax.rem(shift + block - i * TURN, block), 1)
            tiles.append(jnp.where(keep, turned[:, 0:128], 0.0)[None])
        tiles = jnp.concatenate(tiles, axis=0)
        res = jnp.concatenate([res[:, :, 0:128], res[:, :, 128:], tiles], axis=1)
        owner = start // TURN
        send_ref[owner : owner + owners] = res.astype(BF16)


def compact_body(got_ref, out_ref):
    owners = got_ref.shape[0]
    slots = owners * TURN
    got = got_ref[...].astype(F32)
    info = got[:, 2 * TURN :, :].reshape(slots // 128, 128 // TURN, 8, 128)
    info = jnp.sum(info, axis=1)
    info = jnp.concatenate([info[g] for g in range(slots // 128)], axis=1)
    valid = info[TENS : TENS + 1] > 0.0
    before = hot(iota((slots, slots), 0) < iota((slots, slots), 1))
    line = jnp.broadcast_to(valid.astype(F32), (8, slots)).astype(BF16)
    position = jnp.where(valid, dot(line, before)[0:1], -1.0)
    match = hot(iota((slots, slots), 0).astype(F32) == position)
    rows = [got[:, i * TURN : (i + 1) * TURN, :].reshape(slots, 128) for i in range(2)]
    rows = jnp.concatenate(rows, axis=1).astype(BF16)
    limit = out_ref.shape[0] - INFO
    found = dot(match[0:limit], rows)
    packed = dot(info.astype(BF16), match, NT)
    lines = []
    for table in (packed, info):
        for digit in (TENS, ONES):
            lines += [table[digit : digit + 1, 0:256], table[digit : digit + 1, 256:]]
    lines.append(jnp.zeros((INFO - len(lines), 256), F32))
    out_ref[...] = jnp.concatenate([found] + lines, axis=0).astype(BF16)


def turned_lanes(x, core):
    half = x.shape[1] // 2
    return jnp.where(core == 1, jnp.concatenate([x[:, half:], x[:, :half]], axis=1), x)


def window_body(me_ref, core_ref, c0, c1, c2, c3, win_ref, third_ref, place_ref, stack):
    me = me_ref[0]
    for k, ref in enumerate((c0, c1, c2, c3)):
        stack[sender(me, k)] = ref[...]
    limit = stack.shape[1] - INFO
    line = iota((256, limit), 0)
    side = jnp.where(me == 0, 1, me - 1)
    other = jnp.where(me == 0, 3, jnp.where(me == 3, 0, me + 1))
    ranks = jnp.concatenate([line + me * 256, line + side * 256, line + other * 256], axis=0)
    ranks = ranks.astype(F32)
    total = 0.0
    places = []
    for i in range(CHAN):
        info = stack[i, limit:, :].astype(F32)

        def value(at):
            tens = jnp.concatenate([info[at : at + 1], info[at + 1 : at + 2]], axis=1)
            ones = jnp.concatenate([info[at + 2 : at + 3], info[at + 3 : at + 4]], axis=1)
            return tens * 32.0 + ones - 32.0

        places.append(value(4))
        total += dot(hot(ranks == value(0)[:, 0:limit]), stack[i, 0:limit, :])
    places.append(jnp.zeros_like(places[0]))
    place_ref[...] = jnp.concatenate(places + places[4:] * 3, axis=0)
    total = total.astype(BF16)
    win_ref[...] = turned_lanes(total[0:512], core_ref[0])
    third_ref[...] = total[512:]


def pack_body(core_ref, conv_ref, up_ref, down_ref, near_ref, far_ref):
    for mine, dst in ((core_ref[0], near_ref), (1 - core_ref[0], far_ref)):
        half = pl.ds(pl.multiple_of(mine * 128, 128), 128)
        at = conv_ref.shape[0]
        dst[0:at, :] = conv_ref[:, half]
        for ref in (up_ref, down_ref):
            size = ref.shape[1]
            dst[at : at + size, :] = ref[half, :].astype(F32).T.astype(BF16)
            at += size


def weight_reader(near_w, far_w, quarter):
    def weight(k, at, size):
        rows = pl.ds(pl.multiple_of(at, quarter), size)
        return jnp.concatenate([near_w[k][rows, :], far_w[k][rows, :]], axis=1)

    return weight


def rows_at(me, core, k, quarter):
    owner = lax.rem(me + CHAN - k + 2 * core, CHAN)
    return pl.ds(pl.multiple_of(owner * quarter, quarter), quarter)


def add_conv(total, near_ref, cols, rows, weight, quarter):
    near = near_ref[...]
    target = jnp.where(near < 0, -1, near + iota(near.shape, 1))
    target = jnp.concatenate([target.astype(F32), jnp.zeros((5, near.shape[1]), F32)], axis=0).T
    cols = cols.astype(F32)
    group = 3

    def kernel(j):
        return jnp.concatenate([weight(k, j * quarter, quarter) for k in range(CHAN)], axis=0)

    for start in range(0, KER, group):
        js = range(start, start + group)
        match = jnp.concatenate([hot(cols == target[:, j : j + 1]) for j in js], axis=0)
        picked = dot(match, rows).astype(BF16)
        picked = jnp.concatenate([picked[i * 256 : (i + 1) * 256] for i in range(group)], axis=1)
        total += dot(jnp.concatenate([kernel(j) for j in js], axis=1), picked, NT)
    return total


def conv_first_body(me_ref, core_ref, win_ref, near_ref, *refs):
    near_w, far_w, out_ref, turned = refs[0:4], refs[4:8], refs[8], refs[9]
    me, core = me_ref[0], core_ref[0]
    quarter = 64
    turned[...] = win_ref[0:256, :].astype(F32).T
    own = [turned[rows_at(me, core, k, quarter), :] for k in range(CHAN)]
    lane = iota((256, 512), 1)
    cols = jnp.where(lane < 256, lane + 256, jnp.where(me == 0, lane + 256, lane - 256))
    weight = weight_reader(near_w, far_w, quarter)
    out_ref[...] = add_conv(
        jnp.concatenate(own, axis=0), near_ref, cols, win_ref[...], weight, quarter
    )


def conv_second_body(me_ref, core_ref, acc_ref, halo_ref, third_ref, near_ref, *refs):
    near_w, far_w, outs, norm_ref = refs[0:4], refs[4:8], refs[8:12], refs[12]
    me, core = me_ref[0], core_ref[0]
    quarter = 64
    whole = CHAN * quarter
    half = whole // 2
    weight = weight_reader(near_w, far_w, quarter)
    edge = (me == 0) | (me == CHAN - 1)
    rows = turned_lanes(jnp.where(edge, halo_ref[...], third_ref[...]), core)
    cols = iota((256, 256), 1) + jnp.where(me == 0, 0, 512)
    second = add_conv(acc_ref[...], near_ref, cols, rows, weight, quarter).astype(BF16)
    norm = column_norm(second.astype(F32))
    for k in range(CHAN):
        norm_ref[rows_at(me, core, k, quarter), :] = norm[k * quarter : (k + 1) * quarter]
    total = second.astype(F32)
    lo, hi = half * core, half * (1 - core)
    up_at = KER * quarter
    down_at = up_at + whole
    for k in range(CHAN):
        up = [weight(k, up_at + x, half) for x in (lo, hi)]
        hidden = dot(jnp.concatenate(up, axis=0), norm_ref[...])
        hidden = (0.5 * hidden * (1.0 + lax.erf(hidden * (2.0 ** -0.5)))).astype(BF16)
        down = [weight(k, down_at + sender(me, p) * quarter, quarter) for p in range(CHAN)]
        total += dot(jnp.concatenate(down, axis=0), hidden)
    third = total.astype(BF16)
    for k in range(CHAN):
        p = (CHAN - k) % CHAN
        outs[k][...] = third[p * quarter : (p + 1) * quarter]


def back_body(me_ref, t0, t1, t2, t3, place_ref, out_ref, tmp):
    me = me_ref[0]
    for k, ref in enumerate((t0, t1, t2, t3)):
        tmp[sender(me, k)] = ref[...]
    third = jnp.concatenate([tmp[q] for q in range(CHAN)], axis=1)
    zero = jnp.zeros_like(third)
    low = jnp.concatenate([third, zero], axis=0)
    high = jnp.concatenate([zero, third], axis=0)
    column = place_ref[...].T
    slots = column.shape[0]
    block = 256
    rank = iota((block, third.shape[1]), 1).astype(F32)
    for start in range(0, slots, block):
        res = []
        for odd in range(2):
            part = 0.0
            for half, rhs in enumerate((low, high)):
                i = 2 * half + odd
                part += dot(hot(rank == column[start : start + block, i : i + 1]), rhs, NT)
            res.append(part.reshape(block // TURN, TURN, 128))
        owner = start // TURN
        out_ref[owner : owner + block // TURN] = jnp.concatenate(res, axis=1).astype(BF16)


def restore_body(got_ref, codes_ref, out_ref):
    width, rows = out_ref.shape
    got = got_ref[...].reshape(-1, 2 * width).astype(F32).T.astype(BF16)
    code = codes_ref[0:1, :]
    res = 0.0
    for half in range(2):
        for start in range(0, got.shape[1], 256):
            match = hot(iota((256, rows), 0) + (start + half * rows) == code)
            res += dot(got[half * width : (half + 1) * width, start : start + 256], match)
    out_ref[...] = res.astype(BF16)


def turn(k):
    return [(i, (i + k) % CHAN) for i in range(CHAN)]


def gather_chan(x):
    return [x] + [lax.ppermute(x, "chan", turn(k)) for k in range(1, CHAN)]


def exchange(parts):
    return lax.all_to_all(parts, "range", split_axis=0, concat_axis=0, tiled=True)


def shards(
    features, hilbert_rank, neighbours, qkv_weight, out_weight, conv_weight, up_weight, down_weight
):
    quarter, rows = features.shape
    whole = CHAN * quarter
    owners = lax.axis_size("range")
    me = lax.axis_index("chan").astype(I32)
    position = lax.axis_index("range").astype(I32)
    core = lax.rem(position, 2)
    me_ref, core_ref, range_ref = me[None], core[None], position[None]
    swap = [(i, i ^ 1) for i in range(owners)]
    sds = jax.ShapeDtypeStruct
    vmem = pltpu.VMEM

    with jax.named_scope("gather_features"):
        qkv = jnp.transpose(qkv_weight, (0, 2, 1)).reshape(3 * quarter, whole)
        merged = kernel_call(
            merge_body,
            sds((2 * quarter, rows), BF16),
            1 << 20,
            [features, qkv, out_weight.T],
            managed=True,
        )
        blocks = gather_chan(merged)
    with jax.named_scope("codes"):
        codes = kernel_call(
            functools.partial(code_body, owners),
            sds((8, rows), I32),
            1 << 20,
            [me_ref, hilbert_rank[None, :]],
        )
    with jax.named_scope("gather_weights"):
        size = KER * quarter + 2 * up_weight.shape[1]
        near0, far0 = kernel_call(
            pack_body,
            (sds((size, 128), BF16), sds((size, 128), BF16)),
            1 << 20,
            [core_ref, conv_weight.reshape(KER * quarter, whole), up_weight, down_weight],
        )
        blocks, codes, near0, far0 = lax.optimization_barrier((blocks, codes, near0, far0))
        near_w = gather_chan(near0)
        far_w = [far0] + [lax.ppermute(w, "range", swap) for w in near_w[1:]]
    with jax.named_scope("attention"):
        send = kernel_call(
            attention_body,
            sds((owners, 3 * TURN, 128), BF16),
            1 << 32,
            [me_ref, range_ref] + blocks + [codes],
            [
                vmem((whole, rows), BF16),
                vmem((CHAN, quarter, rows), BF16),
                vmem((whole, rows // CHAN), BF16),
            ],
        )
    with jax.named_scope("exchange"):
        got = exchange(send)
        got, far_w = lax.optimization_barrier((got, far_w))
    with jax.named_scope("compact"):
        limit = (rows + (CHAN - 1) * owners) // CHAN
        limit = (limit + 15) // 16 * 16
        found = kernel_call(compact_body, sds((limit + INFO, whole), BF16), 1 << 28, [got])
        found = gather_chan(found)
        found, far_w = lax.optimization_barrier((found, far_w))
    with jax.named_scope("window"):
        win, third, place = kernel_call(
            window_body,
            (sds((512, whole), BF16), sds((256, whole), BF16), sds((8, owners * TURN), F32)),
            1 << 28,
            [me_ref, core_ref] + found,
            [vmem((CHAN, limit + INFO, whole), BF16)],
        )
        pairs = [(i * CHAN, (i + 1) * CHAN) for i in range(owners - 1)]
        pairs += [((i + 1) * CHAN + CHAN - 1, i * CHAN + CHAN - 1) for i in range(owners - 1)]
        halo = lax.ppermute(third, ("range", "chan"), pairs)
    with jax.named_scope("conv"):
        near_ranks = lax.dynamic_slice_in_dim(neighbours, me * 256, 256, 1)
        acc = kernel_call(
            conv_first_body,
            sds((whole, 256), F32),
            1 << 32,
            [me_ref, core_ref, win, near_ranks] + near_w + far_w,
            [vmem((whole, 256), F32)],
        )
        edge = sds((quarter, 256), BF16)
        thirds = kernel_call(
            conv_second_body,
            (edge, edge, edge, edge),
            1 << 32,
            [me_ref, core_ref, acc, halo, third, near_ranks] + near_w + far_w,
            [vmem((whole, 256), BF16)],
        )
    with jax.named_scope("turn_back"):
        thirds = [thirds[0]] + [lax.ppermute(thirds[k], "chan", turn(k)) for k in range(1, CHAN)]
    with jax.named_scope("back"):
        back = kernel_call(
            back_body,
            sds((owners, 2 * TURN, 128), BF16),
            1 << 30,
            [me_ref] + thirds + [place],
            [vmem((CHAN, quarter, 256), BF16)],
        )
        returned = exchange(back)
    with jax.named_scope("restore"):
        return kernel_call(restore_body, sds((quarter, rows), BF16), 1 << 30, [returned, codes])


def solution(mesh):
    in_specs = (
        P("chan", "range"),
        P("range"),
        P(None, "range"),
        P(None, None, "chan"),
        P(None, "chan"),
        P(None, "chan", None),
        P(None, "chan"),
        P("chan", None),
    )
    out_specs = P("chan", "range")
    return jax.shard_map(shards, mesh=mesh, in_specs=in_specs, out_specs=out_specs, check_vma=False)
```

```python
import functools

import jax
import jax.numpy as jnp
from jax import lax
from jax.experimental import pallas as pl
from jax.experimental.pallas import tpu as pltpu
from jax.sharding import PartitionSpec as P

HD = 16
KER = 27
HW = 256
CHAN = 4
SLOTS = 32
TURN = SLOTS // CHAN
INFO = 16
TENS = 4
ONES = 5
F32 = jnp.float32
BF16 = jnp.bfloat16
I32 = jnp.int32

NN = (((1,), (0,)), ((), ()))
NT = (((1,), (1,)), ((), ()))
TN = (((0,), (0,)), ((), ()))


def dot(a, b, dims=NN):
    return lax.dot_general(a, b, dims, preferred_element_type=F32)


def iota(shape, axis):
    return lax.broadcasted_iota(I32, shape, axis)


def hot(mask):
    return mask.astype(F32).astype(BF16)


def kernel_call(body, outs, cost, operands, scratch=(), vmem=24, managed=False):
    place = None if managed else pltpu.VMEM
    vmem = 62 if managed else vmem
    specs = [pl.BlockSpec(memory_space=pltpu.SMEM if x.shape == (1,) else place) for x in operands]
    call = pl.pallas_call(
        body,
        out_shape=outs,
        in_specs=specs,
        scratch_shapes=list(scratch),
        compiler_params=pltpu.CompilerParams(vmem_limit_bytes=vmem * 1024 * 1024),
        cost_estimate=pl.CostEstimate(flops=cost, bytes_accessed=1 << 20, transcendentals=0),
    )
    return call(*operands)


def column_norm(x):
    mean = jnp.mean(x, axis=0, keepdims=True)
    centred = x - mean
    var = jnp.mean(centred * centred, axis=0, keepdims=True)
    return (centred * lax.rsqrt(var + 1e-05)).astype(BF16)


def sender(me, k):
    return lax.rem(me + CHAN - k, CHAN)


def code_body(owners, me_ref, rank_ref, out_ref):
    rank = rank_ref[...]
    rows = rank.shape[1]
    owner = rank // rows
    local = rank % rows
    onehot = (iota((owners, rows), 0) == owner).astype(F32)
    up_to = hot(iota((rows, rows), 0) <= iota((rows, rows), 1))
    count = dot(onehot.astype(BF16), up_to)
    below = hot(iota((owners, owners), 1) < iota((owners, owners), 0))
    start = dot(below, count[:, rows - 128 :].astype(BF16))[:, 127:128]
    begin = jnp.sum(onehot * start, axis=0, keepdims=True).astype(I32)
    place = jnp.sum(onehot * (start + count - 1.0), axis=0, keepdims=True).astype(I32)
    turn = place % CHAN
    row = place // CHAN
    slot = row - (begin - turn + CHAN - 1) // CHAN
    back = (turn // 2) * rows + owner * (2 * TURN) + (turn % 2) * TURN + slot
    mine = jnp.where(turn == me_ref[0], row, -1)
    lines = (back, mine, owner, slot, local // 32 + 1, local % 32)
    out_ref[...] = jnp.concatenate(lines + (back, back), axis=0)


def merge_body(x_ref, qkv_ref, out_w_ref, out_ref):
    quarter, rows = x_ref.shape
    whole = qkv_ref.shape[1]
    out_ref[0:quarter, :] = x_ref[...]
    for part in range(3):
        cut = slice(part * quarter, (part + 1) * quarter)
        out_ref[quarter:, part * whole : (part + 1) * whole] = qkv_ref[cut, :]
    out_ref[quarter:, 3 * whole :] = out_w_ref[...]


def attention_body(me_ref, range_ref, *refs):
    blocks = refs[0:4]
    codes_ref, send_ref, xs, ws, heads = refs[4:9]
    me = me_ref[0]
    quarter = blocks[0].shape[0] // 2
    for k in range(CHAN):
        owner = sender(me, k)
        xs[pl.ds(pl.multiple_of(owner * quarter, quarter), quarter), :] = blocks[k][0:quarter, :]
        ws[owner] = blocks[k][quarter:, :]

    codes = codes_ref[...]
    width, rows = xs.shape

    def weight(part):
        cut = slice(part * width, (part + 1) * width)
        return jnp.concatenate([ws[i, :, cut] for i in range(CHAN)], axis=0)

    mine = rows // CHAN
    x = xs[...]
    norm = column_norm(x.astype(F32))
    pick = hot(iota((mine, rows), 0) == codes[1:2])
    own = dot(x, pick, NT)
    own_norm = dot(norm, pick, NT).astype(BF16)
    digits = dot(codes.astype(F32).astype(BF16), pick, NT)
    q = (dot(weight(0), own_norm).astype(BF16) * BF16(0.25)).astype(BF16)
    keys = dot(weight(1), norm).astype(BF16)
    vals = dot(weight(2), norm).astype(BF16)
    ones = hot(iota((HD, rows), 0) == 0)

    def scored(lo):
        at = slice(lo, lo + HD)
        scores = dot(q[at], keys[at], TN)
        return scores, jnp.max(scores, axis=1, keepdims=True)

    scores, top = scored(0)
    for lo in range(0, width, HD):
        later = scored(lo + HD) if lo + HD < width else (None, None)
        at = slice(lo, lo + HD)
        expo = jnp.exp(scores - top).astype(BF16)
        res = dot(jnp.concatenate([vals[at], ones], axis=0), expo, NT)
        heads[at, :] = (res[0:HD] / res[HD : HD + 1]).astype(BF16)
        scores, top = later
    first = (own + dot(weight(3), heads[...])).astype(BF16)

    target = digits[2:3] * TURN + digits[3:4]
    low_digits = digits.astype(BF16)
    shift = lax.rem(range_ref[0], 128 // TURN) * TURN
    lane = iota((8, 128), 1)
    keep = (lane >= shift) & (lane < shift + TURN)
    block = 256
    owners = block // TURN
    for start in range(0, send_ref.shape[0] * TURN, block):
        match = hot((iota((block, mine), 0) + start).astype(F32) == target)
        res = dot(match, first, NT).reshape(owners, TURN, width)
        info = dot(low_digits, match, NT)
        tiles = []
        for i in range(owners):
            turned = pltpu.roll(info, lax.rem(shift + block - i * TURN, block), 1)
            tiles.append(jnp.where(keep, turned[:, 0:128], 0.0)[None])
        tiles = jnp.concatenate(tiles, axis=0)
        res = jnp.concatenate([res[:, :, 0:128], res[:, :, 128:], tiles], axis=1)
        owner = start // TURN
        send_ref[owner : owner + owners] = res.astype(BF16)


def compact_body(got_ref, out_ref):
    owners = got_ref.shape[0]
    slots = owners * TURN
    got = got_ref[...].astype(F32)
    info = got[:, 2 * TURN :, :].reshape(slots // 128, 128 // TURN, 8, 128)
    info = jnp.sum(info, axis=1)
    info = jnp.concatenate([info[g] for g in range(slots // 128)], axis=1)
    valid = info[TENS : TENS + 1] > 0.0
    before = hot(iota((slots, slots), 0) < iota((slots, slots), 1))
    line = jnp.broadcast_to(valid.astype(F32), (8, slots)).astype(BF16)
    position = jnp.where(valid, dot(line, before)[0:1], -1.0)
    match = hot(iota((slots, slots), 0).astype(F32) == position)
    rows = [got[:, i * TURN : (i + 1) * TURN, :].reshape(slots, 128) for i in range(2)]
    rows = jnp.concatenate(rows, axis=1).astype(BF16)
    limit = out_ref.shape[0] - INFO
    found = dot(match[0:limit], rows)
    packed = dot(info.astype(BF16), match, NT)
    lines = []
    for table in (packed, info):
        for digit in (TENS, ONES):
            lines += [table[digit : digit + 1, 0:256], table[digit : digit + 1, 256:]]
    lines.append(jnp.zeros((INFO - len(lines), 256), F32))
    out_ref[...] = jnp.concatenate([found] + lines, axis=0).astype(BF16)


def turned_lanes(x, core):
    half = x.shape[1] // 2
    return jnp.where(core == 1, jnp.concatenate([x[:, half:], x[:, :half]], axis=1), x)


def window_body(me_ref, core_ref, c0, c1, c2, c3, win_ref, third_ref, place_ref, stack):
    me = me_ref[0]
    for k, ref in enumerate((c0, c1, c2, c3)):
        stack[sender(me, k)] = ref[...]
    limit = stack.shape[1] - INFO
    line = iota((256, limit), 0)
    side = jnp.where(me == 0, 1, me - 1)
    other = jnp.where(me == 0, 3, jnp.where(me == 3, 0, me + 1))
    ranks = jnp.concatenate([line + me * 256, line + side * 256, line + other * 256], axis=0)
    ranks = ranks.astype(F32)
    total = 0.0
    places = []
    for i in range(CHAN):
        info = stack[i, limit:, :].astype(F32)

        def value(at):
            tens = jnp.concatenate([info[at : at + 1], info[at + 1 : at + 2]], axis=1)
            ones = jnp.concatenate([info[at + 2 : at + 3], info[at + 3 : at + 4]], axis=1)
            return tens * 32.0 + ones - 32.0

        places.append(value(4))
        total += dot(hot(ranks == value(0)[:, 0:limit]), stack[i, 0:limit, :])
    places.append(jnp.zeros_like(places[0]))
    place_ref[...] = jnp.concatenate(places + places[4:] * 3, axis=0)
    total = total.astype(BF16)
    win_ref[...] = turned_lanes(total[0:512], core_ref[0])
    third_ref[...] = total[512:]


def pack_body(core_ref, conv_ref, up_ref, down_ref, near_ref, far_ref):
    for mine, dst in ((core_ref[0], near_ref), (1 - core_ref[0], far_ref)):
        half = pl.ds(pl.multiple_of(mine * 128, 128), 128)
        at = conv_ref.shape[0]
        dst[0:at, :] = conv_ref[:, half]
        for ref in (up_ref, down_ref):
            size = ref.shape[1]
            dst[at : at + size, :] = ref[half, :].astype(F32).T.astype(BF16)
            at += size


def weight_reader(near_w, far_w, quarter):
    def weight(k, at, size):
        rows = pl.ds(pl.multiple_of(at, quarter), size)
        return jnp.concatenate([near_w[k][rows, :], far_w[k][rows, :]], axis=1)

    return weight


def rows_at(me, core, k, quarter):
    owner = lax.rem(me + CHAN - k + 2 * core, CHAN)
    return pl.ds(pl.multiple_of(owner * quarter, quarter), quarter)


def add_conv(total, near_ref, cols, rows, weight, quarter):
    near = near_ref[...]
    target = jnp.where(near < 0, -1, near + iota(near.shape, 1))
    target = jnp.concatenate([target.astype(F32), jnp.zeros((5, near.shape[1]), F32)], axis=0).T
    cols = cols.astype(F32)
    group = 3

    def kernel(j):
        return jnp.concatenate([weight(k, j * quarter, quarter) for k in range(CHAN)], axis=0)

    for start in range(0, KER, group):
        js = range(start, start + group)
        match = jnp.concatenate([hot(cols == target[:, j : j + 1]) for j in js], axis=0)
        picked = dot(match, rows).astype(BF16)
        picked = jnp.concatenate([picked[i * 256 : (i + 1) * 256] for i in range(group)], axis=1)
        total += dot(jnp.concatenate([kernel(j) for j in js], axis=1), picked, NT)
    return total


def conv_first_body(me_ref, core_ref, win_ref, near_ref, *refs):
    near_w, far_w, out_ref, turned = refs[0:4], refs[4:8], refs[8], refs[9]
    me, core = me_ref[0], core_ref[0]
    quarter = 64
    turned[...] = win_ref[0:256, :].astype(F32).T
    own = [turned[rows_at(me, core, k, quarter), :] for k in range(CHAN)]
    lane = iota((256, 512), 1)
    cols = jnp.where(lane < 256, lane + 256, jnp.where(me == 0, lane + 256, lane - 256))
    weight = weight_reader(near_w, far_w, quarter)
    out_ref[...] = add_conv(
        jnp.concatenate(own, axis=0), near_ref, cols, win_ref[...], weight, quarter
    )


def conv_second_body(me_ref, core_ref, acc_ref, halo_ref, third_ref, near_ref, *refs):
    near_w, far_w, outs, norm_ref = refs[0:4], refs[4:8], refs[8:12], refs[12]
    me, core = me_ref[0], core_ref[0]
    quarter = 64
    whole = CHAN * quarter
    half = whole // 2
    weight = weight_reader(near_w, far_w, quarter)
    edge = (me == 0) | (me == CHAN - 1)
    rows = turned_lanes(jnp.where(edge, halo_ref[...], third_ref[...]), core)
    cols = iota((256, 256), 1) + jnp.where(me == 0, 0, 512)
    second = add_conv(acc_ref[...], near_ref, cols, rows, weight, quarter).astype(BF16)
    norm = column_norm(second.astype(F32))
    for k in range(CHAN):
        norm_ref[rows_at(me, core, k, quarter), :] = norm[k * quarter : (k + 1) * quarter]
    total = second.astype(F32)
    lo, hi = half * core, half * (1 - core)
    up_at = KER * quarter
    down_at = up_at + whole
    for k in range(CHAN):
        up = [weight(k, up_at + x, half) for x in (lo, hi)]
        hidden = dot(jnp.concatenate(up, axis=0), norm_ref[...])
        hidden = (0.5 * hidden * (1.0 + lax.erf(hidden * (2.0 ** -0.5)))).astype(BF16)
        down = [weight(k, down_at + sender(me, p) * quarter, quarter) for p in range(CHAN)]
        total += dot(jnp.concatenate(down, axis=0), hidden)
    third = total.astype(BF16)
    for k in range(CHAN):
        p = (CHAN - k) % CHAN
        outs[k][...] = third[p * quarter : (p + 1) * quarter]


def back_body(me_ref, t0, t1, t2, t3, place_ref, out_ref, tmp):
    me = me_ref[0]
    for k, ref in enumerate((t0, t1, t2, t3)):
        tmp[sender(me, k)] = ref[...]
    third = jnp.concatenate([tmp[q] for q in range(CHAN)], axis=1)
    slots = place_ref.shape[1]
    rank = iota((third.shape[1], slots), 0).astype(F32)
    res = [dot(third, hot(rank == place_ref[i : i + 1, :])) for i in range(CHAN)]
    res = [jnp.concatenate([res[i], res[i + 2]], axis=0).T for i in range(2)]
    res = [x.reshape(slots // TURN, TURN, x.shape[1]) for x in res]
    out_ref[...] = jnp.concatenate(res, axis=1).astype(BF16)


def restore_body(got_ref, codes_ref, out_ref):
    width, rows = out_ref.shape
    got = got_ref[...].reshape(-1, 2 * width).astype(F32).T.astype(BF16)
    code = codes_ref[0:1, :]
    res = 0.0
    for half in range(2):
        match = hot(iota((got.shape[1], rows), 0) + half * rows == code)
        res += dot(got[half * width : (half + 1) * width], match)
    out_ref[...] = res.astype(BF16)


def turn(k):
    return [(i, (i + k) % CHAN) for i in range(CHAN)]


def gather_chan(x):
    return [x] + [lax.ppermute(x, "chan", turn(k)) for k in range(1, CHAN)]


def exchange(parts):
    return lax.all_to_all(parts, "range", split_axis=0, concat_axis=0, tiled=True)


def shards(
    features, hilbert_rank, neighbours, qkv_weight, out_weight, conv_weight, up_weight, down_weight
):
    quarter, rows = features.shape
    whole = CHAN * quarter
    owners = lax.axis_size("range")
    me = lax.axis_index("chan").astype(I32)
    position = lax.axis_index("range").astype(I32)
    core = lax.rem(position, 2)
    me_ref, core_ref, range_ref = me[None], core[None], position[None]
    swap = [(i, i ^ 1) for i in range(owners)]
    sds = jax.ShapeDtypeStruct
    vmem = pltpu.VMEM

    with jax.named_scope("gather_features"):
        qkv = jnp.transpose(qkv_weight, (0, 2, 1)).reshape(3 * quarter, whole)
        merged = kernel_call(
            merge_body,
            sds((2 * quarter, rows), BF16),
            1 << 20,
            [features, qkv, out_weight.T],
            managed=True,
        )
        blocks = gather_chan(merged)
    with jax.named_scope("codes"):
        codes = kernel_call(
            functools.partial(code_body, owners),
            sds((8, rows), I32),
            1 << 20,
            [me_ref, hilbert_rank[None, :]],
        )
    with jax.named_scope("gather_weights"):
        size = KER * quarter + 2 * up_weight.shape[1]
        near0, far0 = kernel_call(
            pack_body,
            (sds((size, 128), BF16), sds((size, 128), BF16)),
            1 << 20,
            [core_ref, conv_weight.reshape(KER * quarter, whole), up_weight, down_weight],
        )
        blocks, codes, near0, far0 = lax.optimization_barrier((blocks, codes, near0, far0))
        near_w = gather_chan(near0)
        far_w = [far0] + [lax.ppermute(w, "range", swap) for w in near_w[1:]]
    with jax.named_scope("attention"):
        send = kernel_call(
            attention_body,
            sds((owners, 3 * TURN, 128), BF16),
            1 << 32,
            [me_ref, range_ref] + blocks + [codes],
            [
                vmem((whole, rows), BF16),
                vmem((CHAN, quarter, rows), BF16),
                vmem((whole, rows // CHAN), BF16),
            ],
        )
    with jax.named_scope("exchange"):
        got = exchange(send)
        got, far_w = lax.optimization_barrier((got, far_w))
    with jax.named_scope("compact"):
        limit = (rows + (CHAN - 1) * owners) // CHAN
        limit = (limit + 15) // 16 * 16
        found = kernel_call(compact_body, sds((limit + INFO, whole), BF16), 1 << 28, [got])
        found = gather_chan(found)
        found, far_w = lax.optimization_barrier((found, far_w))
    with jax.named_scope("window"):
        win, third, place = kernel_call(
            window_body,
            (sds((512, whole), BF16), sds((256, whole), BF16), sds((8, owners * TURN), F32)),
            1 << 28,
            [me_ref, core_ref] + found,
            [vmem((CHAN, limit + INFO, whole), BF16)],
        )
        pairs = [(i * CHAN, (i + 1) * CHAN) for i in range(owners - 1)]
        pairs += [((i + 1) * CHAN + CHAN - 1, i * CHAN + CHAN - 1) for i in range(owners - 1)]
        halo = lax.ppermute(third, ("range", "chan"), pairs)
    with jax.named_scope("conv"):
        near_ranks = lax.dynamic_slice_in_dim(neighbours, me * 256, 256, 1)
        acc = kernel_call(
            conv_first_body,
            sds((whole, 256), F32),
            1 << 32,
            [me_ref, core_ref, win, near_ranks] + near_w + far_w,
            [vmem((whole, 256), F32)],
        )
        edge = sds((quarter, 256), BF16)
        thirds = kernel_call(
            conv_second_body,
            (edge, edge, edge, edge),
            1 << 32,
            [me_ref, core_ref, acc, halo, third, near_ranks] + near_w + far_w,
            [vmem((whole, 256), BF16)],
        )
    with jax.named_scope("turn_back"):
        thirds = [thirds[0]] + [lax.ppermute(thirds[k], "chan", turn(k)) for k in range(1, CHAN)]
    with jax.named_scope("back"):
        back = kernel_call(
            back_body,
            sds((owners, 2 * TURN, 128), BF16),
            1 << 30,
            [me_ref] + thirds + [place],
            [vmem((CHAN, quarter, 256), BF16)],
        )
        returned = exchange(back)
    with jax.named_scope("restore"):
        return kernel_call(restore_body, sds((quarter, rows), BF16), 1 << 30, [returned, codes])


def solution(mesh):
    in_specs = (
        P("chan", "range"),
        P("range"),
        P(None, "range"),
        P(None, None, "chan"),
        P(None, "chan"),
        P(None, "chan", None),
        P(None, "chan"),
        P("chan", None),
    )
    out_specs = P("chan", "range")
    return jax.shard_map(shards, mesh=mesh, in_specs=in_specs, out_specs=out_specs, check_vma=False)
```

```python
import functools

import jax
import jax.numpy as jnp
from jax import lax
from jax.experimental import pallas as pl
from jax.experimental.pallas import tpu as pltpu
from jax.sharding import PartitionSpec as P

HD = 16
KER = 27
HW = 256
CHAN = 4
SLOTS = 32
TURN = SLOTS // CHAN
INFO = 16
TENS = 4
ONES = 5
F32 = jnp.float32
BF16 = jnp.bfloat16
I32 = jnp.int32

NN = (((1,), (0,)), ((), ()))
NT = (((1,), (1,)), ((), ()))
TN = (((0,), (0,)), ((), ()))


def dot(a, b, dims=NN):
    return lax.dot_general(a, b, dims, preferred_element_type=F32)


def iota(shape, axis):
    return lax.broadcasted_iota(I32, shape, axis)


def hot(mask):
    return mask.astype(F32).astype(BF16)


def kernel_call(body, outs, cost, operands, scratch=(), vmem=24, managed=False):
    place = None if managed else pltpu.VMEM
    vmem = 62 if managed else vmem
    specs = [pl.BlockSpec(memory_space=pltpu.SMEM if x.shape == (1,) else place) for x in operands]
    call = pl.pallas_call(
        body,
        out_shape=outs,
        in_specs=specs,
        scratch_shapes=list(scratch),
        compiler_params=pltpu.CompilerParams(vmem_limit_bytes=vmem * 1024 * 1024),
        cost_estimate=pl.CostEstimate(flops=cost, bytes_accessed=1 << 20, transcendentals=0),
    )
    return call(*operands)


def column_norm(x):
    mean = jnp.mean(x, axis=0, keepdims=True)
    centred = x - mean
    var = jnp.mean(centred * centred, axis=0, keepdims=True)
    return (centred * lax.rsqrt(var + 1e-05)).astype(BF16)


def sender(me, k):
    return lax.rem(me + CHAN - k, CHAN)


def code_body(owners, me_ref, rank_ref, out_ref):
    rank = rank_ref[...]
    rows = rank.shape[1]
    owner = rank // rows
    local = rank % rows
    onehot = (iota((owners, rows), 0) == owner).astype(F32)
    up_to = hot(iota((rows, rows), 0) <= iota((rows, rows), 1))
    count = dot(onehot.astype(BF16), up_to)
    below = hot(iota((owners, owners), 1) < iota((owners, owners), 0))
    start = dot(below, count[:, rows - 128 :].astype(BF16))[:, 127:128]
    begin = jnp.sum(onehot * start, axis=0, keepdims=True).astype(I32)
    place = jnp.sum(onehot * (start + count - 1.0), axis=0, keepdims=True).astype(I32)
    turn = place % CHAN
    row = place // CHAN
    slot = row - (begin - turn + CHAN - 1) // CHAN
    back = (turn // 2) * rows + owner * (2 * TURN) + (turn % 2) * TURN + slot
    mine = jnp.where(turn == me_ref[0], row, -1)
    lines = (back, mine, owner, slot, local // 32 + 1, local % 32)
    out_ref[...] = jnp.concatenate(lines + (back, back), axis=0)


def merge_body(x_ref, qkv_ref, out_w_ref, out_ref):
    quarter, rows = x_ref.shape
    whole = qkv_ref.shape[1]
    out_ref[0:quarter, :] = x_ref[...]
    for part in range(3):
        cut = slice(part * quarter, (part + 1) * quarter)
        out_ref[quarter:, part * whole : (part + 1) * whole] = qkv_ref[cut, :]
    out_ref[quarter:, 3 * whole :] = out_w_ref[...]


def attention_body(me_ref, range_ref, *refs):
    blocks = refs[0:4]
    codes_ref, send_ref, xs, ws, heads = refs[4:9]
    me = me_ref[0]
    quarter = blocks[0].shape[0] // 2
    for k in range(CHAN):
        owner = sender(me, k)
        xs[pl.ds(pl.multiple_of(owner * quarter, quarter), quarter), :] = blocks[k][0:quarter, :]
        ws[owner] = blocks[k][quarter:, :]

    codes = codes_ref[...]
    width, rows = xs.shape

    def weight(part):
        cut = slice(part * width, (part + 1) * width)
        return jnp.concatenate([ws[i, :, cut] for i in range(CHAN)], axis=0)

    mine = rows // CHAN
    x = xs[...]
    norm = column_norm(x.astype(F32))
    pick = hot(iota((mine, rows), 0) == codes[1:2])
    own = dot(x, pick, NT)
    own_norm = dot(norm, pick, NT).astype(BF16)
    digits = dot(codes.astype(F32).astype(BF16), pick, NT)
    q = (dot(weight(0), own_norm).astype(BF16) * BF16(0.25)).astype(BF16)
    keys = dot(weight(1), norm).astype(BF16)
    vals = dot(weight(2), norm).astype(BF16)
    ones = hot(iota((HD, rows), 0) == 0)

    def scored(lo):
        at = slice(lo, lo + HD)
        scores = dot(q[at], keys[at], TN)
        return scores, jnp.max(scores, axis=1, keepdims=True)

    scores, top = scored(0)
    for lo in range(0, width, HD):
        later = scored(lo + HD) if lo + HD < width else (None, None)
        at = slice(lo, lo + HD)
        expo = jnp.exp(scores - top).astype(BF16)
        res = dot(jnp.concatenate([vals[at], ones], axis=0), expo, NT)
        heads[at, :] = (res[0:HD] / res[HD : HD + 1]).astype(BF16)
        scores, top = later
    first = (own + dot(weight(3), heads[...])).astype(BF16)

    target = digits[2:3] * TURN + digits[3:4]
    low_digits = digits.astype(BF16)
    shift = lax.rem(range_ref[0], 128 // TURN) * TURN
    lane = iota((8, 128), 1)
    keep = (lane >= shift) & (lane < shift + TURN)
    block = 256
    owners = block // TURN
    for start in range(0, send_ref.shape[0] * TURN, block):
        match = hot((iota((block, mine), 0) + start).astype(F32) == target)
        res = dot(match, first, NT).reshape(owners, TURN, width)
        info = dot(low_digits, match, NT)
        tiles = []
        for i in range(owners):
            turned = pltpu.roll(info, lax.rem(shift + block - i * TURN, block), 1)
            tiles.append(jnp.where(keep, turned[:, 0:128], 0.0)[None])
        tiles = jnp.concatenate(tiles, axis=0)
        res = jnp.concatenate([res[:, :, 0:128], res[:, :, 128:], tiles], axis=1)
        owner = start // TURN
        send_ref[owner : owner + owners] = res.astype(BF16)


def compact_body(got_ref, out_ref):
    owners = got_ref.shape[0]
    slots = owners * TURN
    got = got_ref[...].astype(F32)
    info = got[:, 2 * TURN :, :].reshape(slots // 128, 128 // TURN, 8, 128)
    info = jnp.sum(info, axis=1)
    info = jnp.concatenate([info[g] for g in range(slots // 128)], axis=1)
    valid = info[TENS : TENS + 1] > 0.0
    before = hot(iota((slots, slots), 0) < iota((slots, slots), 1))
    line = jnp.broadcast_to(valid.astype(F32), (8, slots)).astype(BF16)
    position = jnp.where(valid, dot(line, before)[0:1], -1.0)
    match = hot(iota((slots, slots), 0).astype(F32) == position)
    rows = [got[:, i * TURN : (i + 1) * TURN, :].reshape(slots, 128) for i in range(2)]
    rows = jnp.concatenate(rows, axis=1).astype(BF16)
    limit = out_ref.shape[0] - INFO
    found = dot(match[0:limit], rows)
    packed = dot(info.astype(BF16), match, NT)
    lines = []
    for table in (packed, info):
        for digit in (TENS, ONES):
            lines += [table[digit : digit + 1, 0:256], table[digit : digit + 1, 256:]]
    lines.append(jnp.zeros((INFO - len(lines), 256), F32))
    out_ref[...] = jnp.concatenate([found] + lines, axis=0).astype(BF16)


def turned_lanes(x, core):
    half = x.shape[1] // 2
    return jnp.where(core == 1, jnp.concatenate([x[:, half:], x[:, :half]], axis=1), x)


def window_body(me_ref, core_ref, c0, c1, c2, c3, win_ref, third_ref, place_ref, stack):
    me = me_ref[0]
    for k, ref in enumerate((c0, c1, c2, c3)):
        stack[sender(me, k)] = ref[...]
    limit = stack.shape[1] - INFO
    line = iota((256, limit), 0)
    side = jnp.where(me == 0, 1, me - 1)
    other = jnp.where(me == 0, 3, jnp.where(me == 3, 0, me + 1))
    ranks = jnp.concatenate([line + me * 256, line + side * 256, line + other * 256], axis=0)
    ranks = ranks.astype(F32)
    total = 0.0
    places = []
    for i in range(CHAN):
        info = stack[i, limit:, :].astype(F32)

        def value(at):
            tens = jnp.concatenate([info[at : at + 1], info[at + 1 : at + 2]], axis=1)
            ones = jnp.concatenate([info[at + 2 : at + 3], info[at + 3 : at + 4]], axis=1)
            return tens * 32.0 + ones - 32.0

        places.append(value(4))
        total += dot(hot(ranks == value(0)[:, 0:limit]), stack[i, 0:limit, :])
    places.append(jnp.zeros_like(places[0]))
    place_ref[...] = jnp.concatenate(places + places[4:] * 3, axis=0)
    total = total.astype(BF16)
    win_ref[...] = turned_lanes(total[0:512], core_ref[0])
    third_ref[...] = total[512:]


def pack_body(core_ref, conv_ref, up_ref, down_ref, near_ref, far_ref):
    for mine, dst in ((core_ref[0], near_ref), (1 - core_ref[0], far_ref)):
        half = pl.ds(pl.multiple_of(mine * 128, 128), 128)
        at = conv_ref.shape[0]
        dst[0:at, :] = conv_ref[:, half]
        for ref in (up_ref, down_ref):
            size = ref.shape[1]
            dst[at : at + size, :] = ref[half, :].astype(F32).T.astype(BF16)
            at += size


def weight_reader(near_w, far_w, quarter):
    def weight(k, at, size):
        rows = pl.ds(pl.multiple_of(at, quarter), size)
        return jnp.concatenate([near_w[k][rows, :], far_w[k][rows, :]], axis=1)

    return weight


def rows_at(me, core, k, quarter):
    owner = lax.rem(me + CHAN - k + 2 * core, CHAN)
    return pl.ds(pl.multiple_of(owner * quarter, quarter), quarter)


def add_conv(total, near_ref, cols, rows, weight, quarter):
    near = near_ref[...]
    target = jnp.where(near < 0, -1, near + iota(near.shape, 1))
    target = jnp.concatenate([target.astype(F32), jnp.zeros((5, near.shape[1]), F32)], axis=0).T
    cols = cols.astype(F32)
    group = 3

    def kernel(j):
        return jnp.concatenate([weight(k, j * quarter, quarter) for k in range(CHAN)], axis=0)

    for start in range(0, KER, group):
        js = range(start, start + group)
        match = jnp.concatenate([hot(cols == target[:, j : j + 1]) for j in js], axis=0)
        picked = dot(match, rows).astype(BF16)
        picked = jnp.concatenate([picked[i * 256 : (i + 1) * 256] for i in range(group)], axis=1)
        total += dot(jnp.concatenate([kernel(j) for j in js], axis=1), picked, NT)
    return total


def conv_first_body(me_ref, core_ref, win_ref, near_ref, *refs):
    near_w, far_w, out_ref, turned = refs[0:4], refs[4:8], refs[8], refs[9]
    me, core = me_ref[0], core_ref[0]
    quarter = 64
    turned[...] = win_ref[0:256, :].astype(F32).T
    own = [turned[rows_at(me, core, k, quarter), :] for k in range(CHAN)]
    lane = iota((256, 512), 1)
    cols = jnp.where(lane < 256, lane + 256, jnp.where(me == 0, lane + 256, lane - 256))
    weight = weight_reader(near_w, far_w, quarter)
    out_ref[...] = add_conv(
        jnp.concatenate(own, axis=0), near_ref, cols, win_ref[...], weight, quarter
    )


def conv_second_body(me_ref, core_ref, acc_ref, halo_ref, third_ref, near_ref, *refs):
    near_w, far_w, outs, norm_ref = refs[0:4], refs[4:8], refs[8:12], refs[12]
    me, core = me_ref[0], core_ref[0]
    quarter = 64
    whole = CHAN * quarter
    half = whole // 2
    weight = weight_reader(near_w, far_w, quarter)
    edge = (me == 0) | (me == CHAN - 1)
    rows = turned_lanes(jnp.where(edge, halo_ref[...], third_ref[...]), core)
    cols = iota((256, 256), 1) + jnp.where(me == 0, 0, 512)
    second = add_conv(acc_ref[...], near_ref, cols, rows, weight, quarter).astype(BF16)
    norm = column_norm(second.astype(F32))
    for k in range(CHAN):
        norm_ref[rows_at(me, core, k, quarter), :] = norm[k * quarter : (k + 1) * quarter]
    total = second.astype(F32)
    lo, hi = half * core, half * (1 - core)
    up_at = KER * quarter
    down_at = up_at + whole
    for k in range(CHAN):
        up = [weight(k, up_at + x, half) for x in (lo, hi)]
        hidden = dot(jnp.concatenate(up, axis=0), norm_ref[...])
        hidden = (0.5 * hidden * (1.0 + lax.erf(hidden * (2.0 ** -0.5)))).astype(BF16)
        down = [weight(k, down_at + sender(me, p) * quarter, quarter) for p in range(CHAN)]
        total += dot(jnp.concatenate(down, axis=0), hidden)
    third = total.astype(BF16)
    for k in range(CHAN):
        p = (CHAN - k) % CHAN
        outs[k][...] = third[p * quarter : (p + 1) * quarter]


def back_body(me_ref, t0, t1, t2, t3, place_ref, out_ref, tmp):
    me = me_ref[0]
    for k, ref in enumerate((t0, t1, t2, t3)):
        tmp[sender(me, k)] = ref[...]
    third = jnp.concatenate([tmp[q] for q in range(CHAN)], axis=1)
    slots = place_ref.shape[1]
    rank = iota((third.shape[1], slots), 0).astype(F32)
    res = [dot(third, hot(rank == place_ref[i : i + 1, :])) for i in range(CHAN)]
    res = [jnp.concatenate([res[i], res[i + 2]], axis=0).T for i in range(2)]
    res = [x.reshape(slots // TURN, TURN, x.shape[1]) for x in res]
    out_ref[...] = jnp.concatenate(res, axis=1).astype(BF16)


def restore_body(got_ref, codes_ref, out_ref):
    width, rows = out_ref.shape
    got = got_ref[...].reshape(-1, 2 * width).astype(F32).T.astype(BF16)
    code = codes_ref[0:1, :]
    res = 0.0
    for half in range(2):
        match = hot(iota((got.shape[1], rows), 0) + half * rows == code)
        res += dot(got[half * width : (half + 1) * width], match)
    out_ref[...] = res.astype(BF16)


def turn(k):
    return [(i, (i + k) % CHAN) for i in range(CHAN)]


def gather_chan(x):
    return [x] + [lax.ppermute(x, "chan", turn(k)) for k in range(1, CHAN)]


def exchange(parts):
    return lax.all_to_all(parts, "range", split_axis=0, concat_axis=0, tiled=True)


def shards(
    features, hilbert_rank, neighbours, qkv_weight, out_weight, conv_weight, up_weight, down_weight
):
    quarter, rows = features.shape
    whole = CHAN * quarter
    owners = lax.axis_size("range")
    me = lax.axis_index("chan").astype(I32)
    position = lax.axis_index("range").astype(I32)
    core = lax.rem(position, 2)
    me_ref, core_ref, range_ref = me[None], core[None], position[None]
    swap = [(i, i ^ 1) for i in range(owners)]
    sds = jax.ShapeDtypeStruct
    vmem = pltpu.VMEM

    with jax.named_scope("gather_features"):
        qkv = jnp.transpose(qkv_weight, (0, 2, 1)).reshape(3 * quarter, whole)
        merged = kernel_call(
            merge_body,
            sds((2 * quarter, rows), BF16),
            1 << 20,
            [features, qkv, out_weight.T],
            managed=True,
        )
        blocks = gather_chan(merged)
    with jax.named_scope("codes"):
        codes = kernel_call(
            functools.partial(code_body, owners),
            sds((8, rows), I32),
            1 << 20,
            [me_ref, hilbert_rank[None, :]],
        )
    with jax.named_scope("gather_weights"):
        size = KER * quarter + 2 * up_weight.shape[1]
        near0, far0 = kernel_call(
            pack_body,
            (sds((size, 128), BF16), sds((size, 128), BF16)),
            1 << 20,
            [core_ref, conv_weight.reshape(KER * quarter, whole), up_weight, down_weight],
        )
        early = (blocks[1], blocks[2], codes, near0, far0)
        blocks[1], blocks[2], codes, near0, far0 = lax.optimization_barrier(early)
        near_w = gather_chan(near0)
        far_w = [far0] + [lax.ppermute(w, "range", swap) for w in near_w[1:]]
    with jax.named_scope("attention"):
        send = kernel_call(
            attention_body,
            sds((owners, 3 * TURN, 128), BF16),
            1 << 32,
            [me_ref, range_ref] + blocks + [codes],
            [
                vmem((whole, rows), BF16),
                vmem((CHAN, quarter, rows), BF16),
                vmem((whole, rows // CHAN), BF16),
            ],
        )
    with jax.named_scope("exchange"):
        got = exchange(send)
        got, far_w = lax.optimization_barrier((got, far_w))
    with jax.named_scope("compact"):
        limit = (rows + (CHAN - 1) * owners) // CHAN
        limit = (limit + 15) // 16 * 16
        found = kernel_call(compact_body, sds((limit + INFO, whole), BF16), 1 << 28, [got])
        found = gather_chan(found)
        found, far_w = lax.optimization_barrier((found, far_w))
    with jax.named_scope("window"):
        win, third, place = kernel_call(
            window_body,
            (sds((512, whole), BF16), sds((256, whole), BF16), sds((8, owners * TURN), F32)),
            1 << 28,
            [me_ref, core_ref] + found,
            [vmem((CHAN, limit + INFO, whole), BF16)],
        )
        pairs = [(i * CHAN, (i + 1) * CHAN) for i in range(owners - 1)]
        pairs += [((i + 1) * CHAN + CHAN - 1, i * CHAN + CHAN - 1) for i in range(owners - 1)]
        halo = lax.ppermute(third, ("range", "chan"), pairs)
    with jax.named_scope("conv"):
        near_ranks = lax.dynamic_slice_in_dim(neighbours, me * 256, 256, 1)
        acc = kernel_call(
            conv_first_body,
            sds((whole, 256), F32),
            1 << 32,
            [me_ref, core_ref, win, near_ranks] + near_w + far_w,
            [vmem((whole, 256), F32)],
        )
        edge = sds((quarter, 256), BF16)
        thirds = kernel_call(
            conv_second_body,
            (edge, edge, edge, edge),
            1 << 32,
            [me_ref, core_ref, acc, halo, third, near_ranks] + near_w + far_w,
            [vmem((whole, 256), BF16)],
        )
    with jax.named_scope("turn_back"):
        thirds = [thirds[0]] + [lax.ppermute(thirds[k], "chan", turn(k)) for k in range(1, CHAN)]
    with jax.named_scope("back"):
        back = kernel_call(
            back_body,
            sds((owners, 2 * TURN, 128), BF16),
            1 << 30,
            [me_ref] + thirds + [place],
            [vmem((CHAN, quarter, 256), BF16)],
        )
        returned = exchange(back)
    with jax.named_scope("restore"):
        return kernel_call(restore_body, sds((quarter, rows), BF16), 1 << 30, [returned, codes])


def solution(mesh):
    in_specs = (
        P("chan", "range"),
        P("range"),
        P(None, "range"),
        P(None, None, "chan"),
        P(None, "chan"),
        P(None, "chan", None),
        P(None, "chan"),
        P("chan", None),
    )
    out_specs = P("chan", "range")
    return jax.shard_map(shards, mesh=mesh, in_specs=in_specs, out_specs=out_specs, check_vma=False)
```

```python
import functools

import jax
import jax.numpy as jnp
from jax import lax
from jax.experimental import pallas as pl
from jax.experimental.pallas import tpu as pltpu
from jax.sharding import PartitionSpec as P

HD = 16
KER = 27
HW = 256
CHAN = 4
SLOTS = 32
TURN = SLOTS // CHAN
INFO = 16
TENS = 4
ONES = 5
F32 = jnp.float32
BF16 = jnp.bfloat16
I32 = jnp.int32

NN = (((1,), (0,)), ((), ()))
NT = (((1,), (1,)), ((), ()))
TN = (((0,), (0,)), ((), ()))


def dot(a, b, dims=NN):
    return lax.dot_general(a, b, dims, preferred_element_type=F32)


def iota(shape, axis):
    return lax.broadcasted_iota(I32, shape, axis)


def hot(mask):
    return mask.astype(F32).astype(BF16)


def kernel_call(body, outs, cost, operands, scratch=(), vmem=24, managed=False):
    place = None if managed else pltpu.VMEM
    vmem = 62 if managed else vmem
    specs = [pl.BlockSpec(memory_space=pltpu.SMEM if x.shape == (1,) else place) for x in operands]
    call = pl.pallas_call(
        body,
        out_shape=outs,
        in_specs=specs,
        scratch_shapes=list(scratch),
        compiler_params=pltpu.CompilerParams(vmem_limit_bytes=vmem * 1024 * 1024),
        cost_estimate=pl.CostEstimate(flops=cost, bytes_accessed=1 << 20, transcendentals=0),
    )
    return call(*operands)


def column_norm(x):
    mean = jnp.mean(x, axis=0, keepdims=True)
    centred = x - mean
    var = jnp.mean(centred * centred, axis=0, keepdims=True)
    return (centred * lax.rsqrt(var + 1e-05)).astype(BF16)


def sender(me, k):
    return lax.rem(me + CHAN - k, CHAN)


def code_body(owners, me_ref, rank_ref, out_ref):
    rank = rank_ref[...]
    rows = rank.shape[1]
    owner = rank // rows
    local = rank % rows
    onehot = (iota((owners, rows), 0) == owner).astype(F32)
    up_to = hot(iota((rows, rows), 0) <= iota((rows, rows), 1))
    count = dot(onehot.astype(BF16), up_to)
    below = hot(iota((owners, owners), 1) < iota((owners, owners), 0))
    start = dot(below, count[:, rows - 128 :].astype(BF16))[:, 127:128]
    begin = jnp.sum(onehot * start, axis=0, keepdims=True).astype(I32)
    place = jnp.sum(onehot * (start + count - 1.0), axis=0, keepdims=True).astype(I32)
    turn = place % CHAN
    row = place // CHAN
    slot = row - (begin - turn + CHAN - 1) // CHAN
    back = (turn // 2) * rows + owner * (2 * TURN) + (turn % 2) * TURN + slot
    mine = jnp.where(turn == me_ref[0], row, -1)
    lines = (back, mine, owner, slot, local // 32 + 1, local % 32)
    out_ref[...] = jnp.concatenate(lines + (back, back), axis=0)


def merge_body(x_ref, qkv_ref, out_w_ref, out_ref):
    quarter, rows = x_ref.shape
    whole = qkv_ref.shape[1]
    out_ref[0:quarter, :] = x_ref[...]
    for part in range(3):
        cut = slice(part * quarter, (part + 1) * quarter)
        out_ref[quarter:, part * whole : (part + 1) * whole] = qkv_ref[cut, :]
    out_ref[quarter:, 3 * whole :] = out_w_ref[...]


def attention_body(me_ref, range_ref, *refs):
    blocks = refs[0:4]
    codes_ref, send_ref, xs, ws, heads = refs[4:9]
    me = me_ref[0]
    quarter = blocks[0].shape[0] // 2
    for k in range(CHAN):
        owner = sender(me, k)
        xs[pl.ds(pl.multiple_of(owner * quarter, quarter), quarter), :] = blocks[k][0:quarter, :]
        ws[owner] = blocks[k][quarter:, :]

    codes = codes_ref[...]
    width, rows = xs.shape

    def weight(part):
        cut = slice(part * width, (part + 1) * width)
        return jnp.concatenate([ws[i, :, cut] for i in range(CHAN)], axis=0)

    mine = rows // CHAN
    x = xs[...]
    norm = column_norm(x.astype(F32))
    pick = hot(iota((mine, rows), 0) == codes[1:2])
    own = dot(x, pick, NT)
    own_norm = dot(norm, pick, NT).astype(BF16)
    digits = dot(codes.astype(F32).astype(BF16), pick, NT)
    q = (dot(weight(0), own_norm).astype(BF16) * BF16(0.25)).astype(BF16)
    keys = dot(weight(1), norm).astype(BF16)
    vals = dot(weight(2), norm).astype(BF16)
    ones = hot(iota((HD, rows), 0) == 0)

    def scored(lo):
        at = slice(lo, lo + HD)
        scores = dot(q[at], keys[at], TN)
        return scores, jnp.max(scores, axis=1, keepdims=True)

    scores, top = scored(0)
    for lo in range(0, width, HD):
        later = scored(lo + HD) if lo + HD < width else (None, None)
        at = slice(lo, lo + HD)
        expo = jnp.exp(scores - top).astype(BF16)
        res = dot(jnp.concatenate([vals[at], ones], axis=0), expo, NT)
        heads[at, :] = (res[0:HD] / res[HD : HD + 1]).astype(BF16)
        scores, top = later
    first = (own + dot(weight(3), heads[...])).astype(BF16)

    target = digits[2:3] * TURN + digits[3:4]
    low_digits = digits.astype(BF16)
    shift = lax.rem(range_ref[0], 128 // TURN) * TURN
    lane = iota((8, 128), 1)
    keep = (lane >= shift) & (lane < shift + TURN)
    block = 256
    owners = block // TURN
    for start in range(0, send_ref.shape[0] * TURN, block):
        match = hot((iota((block, mine), 0) + start).astype(F32) == target)
        res = dot(match, first, NT).reshape(owners, TURN, width)
        info = dot(low_digits, match, NT)
        tiles = []
        for i in range(owners):
            turned = pltpu.roll(info, lax.rem(shift + block - i * TURN, block), 1)
            tiles.append(jnp.where(keep, turned[:, 0:128], 0.0)[None])
        tiles = jnp.concatenate(tiles, axis=0)
        res = jnp.concatenate([res[:, :, 0:128], res[:, :, 128:], tiles], axis=1)
        owner = start // TURN
        send_ref[owner : owner + owners] = res.astype(BF16)


def compact_body(got_ref, out_ref):
    owners = got_ref.shape[0]
    slots = owners * TURN
    got = got_ref[...].astype(F32)
    info = got[:, 2 * TURN :, :].reshape(slots // 128, 128 // TURN, 8, 128)
    info = jnp.sum(info, axis=1)
    info = jnp.concatenate([info[g] for g in range(slots // 128)], axis=1)
    valid = info[TENS : TENS + 1] > 0.0
    before = hot(iota((slots, slots), 0) < iota((slots, slots), 1))
    line = jnp.broadcast_to(valid.astype(F32), (8, slots)).astype(BF16)
    position = jnp.where(valid, dot(line, before)[0:1], -1.0)
    match = hot(iota((slots, slots), 0).astype(F32) == position)
    rows = [got[:, i * TURN : (i + 1) * TURN, :].reshape(slots, 128) for i in range(2)]
    rows = jnp.concatenate(rows, axis=1).astype(BF16)
    limit = out_ref.shape[0] - INFO
    found = dot(match[0:limit], rows)
    packed = dot(info.astype(BF16), match, NT)
    lines = []
    for table in (packed, info):
        for digit in (TENS, ONES):
            lines += [table[digit : digit + 1, 0:256], table[digit : digit + 1, 256:]]
    lines.append(jnp.zeros((INFO - len(lines), 256), F32))
    out_ref[...] = jnp.concatenate([found] + lines, axis=0).astype(BF16)


def turned_lanes(x, core):
    half = x.shape[1] // 2
    return jnp.where(core == 1, jnp.concatenate([x[:, half:], x[:, :half]], axis=1), x)


def window_body(me_ref, core_ref, c0, c1, c2, c3, win_ref, third_ref, place_ref, stack):
    me = me_ref[0]
    for k, ref in enumerate((c0, c1, c2, c3)):
        stack[sender(me, k)] = ref[...]
    limit = stack.shape[1] - INFO
    line = iota((256, limit), 0)
    side = jnp.where(me == 0, 1, me - 1)
    other = jnp.where(me == 0, 3, jnp.where(me == 3, 0, me + 1))
    ranks = jnp.concatenate([line + me * 256, line + side * 256, line + other * 256], axis=0)
    ranks = ranks.astype(F32)
    total = 0.0
    places = []
    for i in range(CHAN):
        info = stack[i, limit:, :].astype(F32)

        def value(at):
            tens = jnp.concatenate([info[at : at + 1], info[at + 1 : at + 2]], axis=1)
            ones = jnp.concatenate([info[at + 2 : at + 3], info[at + 3 : at + 4]], axis=1)
            return tens * 32.0 + ones - 32.0

        places.append(value(4))
        total += dot(hot(ranks == value(0)[:, 0:limit]), stack[i, 0:limit, :])
    places.append(jnp.zeros_like(places[0]))
    place_ref[...] = jnp.concatenate(places + places[4:] * 3, axis=0)
    total = total.astype(BF16)
    win_ref[...] = turned_lanes(total[0:512], core_ref[0])
    third_ref[...] = total[512:]


def pack_body(core_ref, conv_ref, up_ref, down_ref, near_ref, far_ref):
    for mine, dst in ((core_ref[0], near_ref), (1 - core_ref[0], far_ref)):
        half = pl.ds(pl.multiple_of(mine * 128, 128), 128)
        at = conv_ref.shape[0]
        dst[0:at, :] = conv_ref[:, half]
        for ref in (up_ref, down_ref):
            size = ref.shape[1]
            dst[at : at + size, :] = ref[half, :].astype(F32).T.astype(BF16)
            at += size


def weight_reader(near_w, far_w, quarter):
    def weight(k, at, size):
        rows = pl.ds(pl.multiple_of(at, quarter), size)
        return jnp.concatenate([near_w[k][rows, :], far_w[k][rows, :]], axis=1)

    return weight


def rows_at(me, core, k, quarter):
    owner = lax.rem(me + CHAN - k + 2 * core, CHAN)
    return pl.ds(pl.multiple_of(owner * quarter, quarter), quarter)


def add_conv(total, near_ref, cols, rows, weight, quarter):
    near = near_ref[...]
    target = jnp.where(near < 0, -1, near + iota(near.shape, 1))
    target = jnp.concatenate([target.astype(F32), jnp.zeros((5, near.shape[1]), F32)], axis=0).T
    cols = cols.astype(F32)
    group = 3

    def kernel(j):
        return jnp.concatenate([weight(k, j * quarter, quarter) for k in range(CHAN)], axis=0)

    for start in range(0, KER, group):
        js = range(start, start + group)
        match = jnp.concatenate([hot(cols == target[:, j : j + 1]) for j in js], axis=0)
        picked = dot(match, rows).astype(BF16)
        picked = jnp.concatenate([picked[i * 256 : (i + 1) * 256] for i in range(group)], axis=1)
        total += dot(jnp.concatenate([kernel(j) for j in js], axis=1), picked, NT)
    return total


def conv_first_body(me_ref, core_ref, win_ref, near_ref, *refs):
    near_w, far_w, out_ref, turned = refs[0:4], refs[4:8], refs[8], refs[9]
    me, core = me_ref[0], core_ref[0]
    quarter = 64
    turned[...] = win_ref[0:256, :].astype(F32).T
    own = [turned[rows_at(me, core, k, quarter), :] for k in range(CHAN)]
    lane = iota((256, 512), 1)
    cols = jnp.where(lane < 256, lane + 256, jnp.where(me == 0, lane + 256, lane - 256))
    weight = weight_reader(near_w, far_w, quarter)
    out_ref[...] = add_conv(
        jnp.concatenate(own, axis=0), near_ref, cols, win_ref[...], weight, quarter
    )


def conv_second_body(me_ref, core_ref, acc_ref, halo_ref, third_ref, near_ref, *refs):
    near_w, far_w, outs, norm_ref = refs[0:4], refs[4:8], refs[8:12], refs[12]
    me, core = me_ref[0], core_ref[0]
    quarter = 64
    whole = CHAN * quarter
    half = whole // 2
    weight = weight_reader(near_w, far_w, quarter)
    edge = (me == 0) | (me == CHAN - 1)
    rows = turned_lanes(jnp.where(edge, halo_ref[...], third_ref[...]), core)
    cols = iota((256, 256), 1) + jnp.where(me == 0, 0, 512)
    second = add_conv(acc_ref[...], near_ref, cols, rows, weight, quarter).astype(BF16)
    norm = column_norm(second.astype(F32))
    for k in range(CHAN):
        norm_ref[rows_at(me, core, k, quarter), :] = norm[k * quarter : (k + 1) * quarter]
    total = second.astype(F32)
    lo, hi = half * core, half * (1 - core)
    up_at = KER * quarter
    down_at = up_at + whole
    for k in range(CHAN):
        up = [weight(k, up_at + x, half) for x in (lo, hi)]
        hidden = dot(jnp.concatenate(up, axis=0), norm_ref[...])
        hidden = (0.5 * hidden * (1.0 + lax.erf(hidden * (2.0 ** -0.5)))).astype(BF16)
        down = [weight(k, down_at + sender(me, p) * quarter, quarter) for p in range(CHAN)]
        total += dot(jnp.concatenate(down, axis=0), hidden)
    third = total.astype(BF16)
    for k in range(CHAN):
        p = (CHAN - k) % CHAN
        outs[k][...] = third[p * quarter : (p + 1) * quarter]


def back_body(me_ref, t0, t1, t2, t3, place_ref, out_ref, tmp):
    me = me_ref[0]
    for k, ref in enumerate((t0, t1, t2, t3)):
        tmp[sender(me, k)] = ref[...]
    third = jnp.concatenate([tmp[q] for q in range(CHAN)], axis=1)
    slots = place_ref.shape[1]
    rank = iota((third.shape[1], slots), 0).astype(F32)
    res = [dot(third, hot(rank == place_ref[i : i + 1, :])) for i in range(CHAN)]
    res = [jnp.concatenate([res[i], res[i + 2]], axis=0).T for i in range(2)]
    res = [x.reshape(slots // TURN, TURN, x.shape[1]) for x in res]
    out_ref[...] = jnp.concatenate(res, axis=1).astype(BF16)


def restore_body(got_ref, codes_ref, out_ref):
    width, rows = out_ref.shape
    got = got_ref[...].reshape(-1, 2 * width).astype(F32).T.astype(BF16)
    code = codes_ref[0:1, :]
    res = 0.0
    for half in range(2):
        match = hot(iota((got.shape[1], rows), 0) + half * rows == code)
        res += dot(got[half * width : (half + 1) * width], match)
    out_ref[...] = res.astype(BF16)


def turn(k):
    return [(i, (i + k) % CHAN) for i in range(CHAN)]


def gather_chan(x):
    return [x] + [lax.ppermute(x, "chan", turn(k)) for k in range(1, CHAN)]


def exchange(parts):
    return lax.all_to_all(parts, "range", split_axis=0, concat_axis=0, tiled=True)


def shards(
    features, hilbert_rank, neighbours, qkv_weight, out_weight, conv_weight, up_weight, down_weight
):
    quarter, rows = features.shape
    whole = CHAN * quarter
    owners = lax.axis_size("range")
    me = lax.axis_index("chan").astype(I32)
    position = lax.axis_index("range").astype(I32)
    core = lax.rem(position, 2)
    me_ref, core_ref, range_ref = me[None], core[None], position[None]
    swap = [(i, i ^ 1) for i in range(owners)]
    sds = jax.ShapeDtypeStruct
    vmem = pltpu.VMEM

    with jax.named_scope("gather_features"):
        qkv = jnp.transpose(qkv_weight, (0, 2, 1)).reshape(3 * quarter, whole)
        merged = kernel_call(
            merge_body,
            sds((2 * quarter, rows), BF16),
            1 << 20,
            [features, qkv, out_weight.T],
            managed=True,
        )
        blocks = gather_chan(merged)
    with jax.named_scope("codes"):
        codes = kernel_call(
            functools.partial(code_body, owners),
            sds((8, rows), I32),
            1 << 20,
            [me_ref, hilbert_rank[None, :]],
        )
    with jax.named_scope("gather_weights"):
        size = KER * quarter + 2 * up_weight.shape[1]
        near0, far0 = kernel_call(
            pack_body,
            (sds((size, 128), BF16), sds((size, 128), BF16)),
            1 << 20,
            [core_ref, conv_weight.reshape(KER * quarter, whole), up_weight, down_weight],
        )
        early = (blocks[2], codes, near0, far0)
        blocks[2], codes, near0, far0 = lax.optimization_barrier(early)
        near_w = gather_chan(near0)
        far_w = [far0] + [lax.ppermute(w, "range", swap) for w in near_w[1:]]
    with jax.named_scope("attention"):
        send = kernel_call(
            attention_body,
            sds((owners, 3 * TURN, 128), BF16),
            1 << 32,
            [me_ref, range_ref] + blocks + [codes],
            [
                vmem((whole, rows), BF16),
                vmem((CHAN, quarter, rows), BF16),
                vmem((whole, rows // CHAN), BF16),
            ],
        )
    with jax.named_scope("exchange"):
        got = exchange(send)
        got, far_w = lax.optimization_barrier((got, far_w))
    with jax.named_scope("compact"):
        limit = (rows + (CHAN - 1) * owners) // CHAN
        limit = (limit + 15) // 16 * 16
        found = kernel_call(compact_body, sds((limit + INFO, whole), BF16), 1 << 28, [got])
        found = gather_chan(found)
        found, far_w = lax.optimization_barrier((found, far_w))
    with jax.named_scope("window"):
        win, third, place = kernel_call(
            window_body,
            (sds((512, whole), BF16), sds((256, whole), BF16), sds((8, owners * TURN), F32)),
            1 << 28,
            [me_ref, core_ref] + found,
            [vmem((CHAN, limit + INFO, whole), BF16)],
        )
        pairs = [(i * CHAN, (i + 1) * CHAN) for i in range(owners - 1)]
        pairs += [((i + 1) * CHAN + CHAN - 1, i * CHAN + CHAN - 1) for i in range(owners - 1)]
        halo = lax.ppermute(third, ("range", "chan"), pairs)
    with jax.named_scope("conv"):
        near_ranks = lax.dynamic_slice_in_dim(neighbours, me * 256, 256, 1)
        acc = kernel_call(
            conv_first_body,
            sds((whole, 256), F32),
            1 << 32,
            [me_ref, core_ref, win, near_ranks] + near_w + far_w,
            [vmem((whole, 256), F32)],
        )
        edge = sds((quarter, 256), BF16)
        thirds = kernel_call(
            conv_second_body,
            (edge, edge, edge, edge),
            1 << 32,
            [me_ref, core_ref, acc, halo, third, near_ranks] + near_w + far_w,
            [vmem((whole, 256), BF16)],
        )
    with jax.named_scope("turn_back"):
        thirds = [thirds[0]] + [lax.ppermute(thirds[k], "chan", turn(k)) for k in range(1, CHAN)]
    with jax.named_scope("back"):
        back = kernel_call(
            back_body,
            sds((owners, 2 * TURN, 128), BF16),
            1 << 30,
            [me_ref] + thirds + [place],
            [vmem((CHAN, quarter, 256), BF16)],
        )
        returned = exchange(back)
    with jax.named_scope("restore"):
        return kernel_call(restore_body, sds((quarter, rows), BF16), 1 << 30, [returned, codes])


def solution(mesh):
    in_specs = (
        P("chan", "range"),
        P("range"),
        P(None, "range"),
        P(None, None, "chan"),
        P(None, "chan"),
        P(None, "chan", None),
        P(None, "chan"),
        P("chan", None),
    )
    out_specs = P("chan", "range")
    return jax.shard_map(shards, mesh=mesh, in_specs=in_specs, out_specs=out_specs, check_vma=False)
```
